512 devices in a mesh: dp: 16 (over y, core), vocab: 32 (over x, z).
Axes of the slice: x: 4, y: 8, z: 8, core: 2. Of those that a mesh axis runs over, the one named last changes fastest.
Arguments:
- states: bfloat16 [8192, 2048], P('dp'), may hold values from -8 to 8
- head_weight: bfloat16 [2048, 65536], P('dp', 'vocab')
- targets: int32 [8192], P('dp'), may hold values from 0 to 65535
- positions: int32 [32, 256], P('dp'), may hold values from 0 to 255, each once within a row
- counts: int32 [32], P('dp'), may hold values from 1 to 48, 896 in all
- rate_num: int32 [32], P('dp'), may hold values from 64 to 1024
Outputs:
- mean_loss: float32 [], replicated
- grad_hidden: bfloat16 [8192, 2048], P('dp', 'vocab')
- grad_weight: float32 [2048, 65536], P('dp', 'vocab')
The draws below stay inside these ranges and needn't reach their ends.
Inputs may be any that keep to these rules, and one draw needn't show every extreme that they name: Largest count is 48; the counts sum to 896. Each row is a permutation of the positions.
All inputs are finite; a program needn't handle non-finite values. No bound on the sum of `counts` on one device may be relied on, other than what follows from the above.
Results may differ from the reference program's by a relative error of at most 0.0044.
Values may be sent and summed in bfloat16 or wider, within the bound.
A program may use at most 64 MiB of HBM per device.

```python
import math
import jax
import jax.numpy as jnp
import numpy as np
from jax import lax

D = 2048
V = 65536
SEQ_LEN = 256
CAP = 48
MEANC = 28
RATE_DEN = 1024
NSEQ = 32
TOKENS = 8192


def shared_columns(key):
    normal_base = jax.random.normal(key, (D, V), jnp.float32) * (3.0 / math.sqrt(D))
    return normal_base


def draw_head_weight(key, part):
    columns = shared_columns(key)
    return columns.astype(jnp.bfloat16)


def draw_states(key, part):
    key = jax.random.fold_in(key, 2)
    sampled = jnp.clip(jax.random.normal(key, (TOKENS, D), jnp.float32), -6.0, 6.0)
    return sampled.astype(jnp.bfloat16)


def set_ends(result, key, least, largest):
    longest = result.shape.index(max(result.shape))
    spots = []
    for shift in (0, 1):
        where = [jax.random.randint(jax.random.fold_in(key, axis), (), 0, length) for axis, length in enumerate(result.shape)]
        where[longest] = (where[longest] + shift) % result.shape[longest]
        spots.append(tuple(where))
    return result.at[spots[0]].set(least).at[spots[1]].set(largest)


def rank_bounds(number_of, skew):
    weights = [(1 << 20) // math.isqrt(rank ** skew) + 1 for rank in range(1, number_of + 1)]
    deviation = 1 + sum(weights) // (1 << 30)
    return np.cumsum(np.array([max(1, weight // deviation) for weight in weights]))


def ranked_ids(own_key, dims, number_of, slope):
    table = rank_bounds(number_of, slope)
    ticket = jax.random.randint(jax.random.fold_in(own_key, 1), dims, 0, int(table[number_of - 1]))
    rank = jnp.searchsorted(jnp.asarray(table, jnp.int32), ticket, side="right")
    return jax.random.permutation(jax.random.fold_in(own_key, 2), number_of)[rank].astype(jnp.int32)


def length_profile(amount, total, limit, slope):
    portions = [(1 << 20) // math.isqrt(standing ** slope) + 1 for standing in range(2, amount + 1)]
    surplus, holding = total - limit - (amount - 1), [1] * (amount - 1)
    while surplus > 0:
        free = [i for i in range(amount - 1) if holding[i] < limit]
        whole, budget = sum([portions[i] for i in free]), surplus
        for i in free:
            addition = min(limit - holding[i], max(1, budget * portions[i] // whole), surplus)
            holding[i] = holding[i] + addition
            surplus = surplus - addition
    return np.array([limit] + holding)


def uneven(stream_key, count, total, bound, skew):
    if count == 2:
        one = jax.random.randint(stream_key, (), max(1, total - bound), min(bound, total - 1) + 1)
        return jnp.stack([one, total - one])
    tallies = jnp.asarray(length_profile(count, total, bound, skew), jnp.int32)
    couples = (count - 1) // 2
    giver, receiver = tallies[1:1 + 2 * couples:2], tallies[2:2 + 2 * couples:2]
    slack = jnp.minimum(giver - 1, bound - receiver)
    shifted = jax.random.randint(jax.random.fold_in(stream_key, 1), (couples,), 0, 1 << 20) % (slack + 1)
    tallies = tallies.at[1:1 + 2 * couples:2].set(giver - shifted).at[2:2 + 2 * couples:2].set(receiver + shifted)
    return tallies[jax.random.permutation(jax.random.fold_in(stream_key, 2), count)]


def setup_inputs(seed: int = 0) -> dict:
    splits = jax.random.split(jax.random.key(seed), 7)
    states = draw_states(jax.random.fold_in(splits[6], 71), 0)
    head_weight = draw_head_weight(jax.random.fold_in(splits[6], 71), 0)
    targets = set_ends(ranked_ids(splits[2], (TOKENS,), V, 2), jax.random.fold_in(splits[2], 3), 0, V - 1).astype(jnp.int32)
    positions = jax.vmap(lambda own: jax.random.permutation(own, SEQ_LEN))(jax.random.split(splits[3], NSEQ)).reshape((NSEQ, SEQ_LEN)).astype(jnp.int32)
    counts = uneven(splits[4], NSEQ, NSEQ * MEANC, CAP, 2).astype(jnp.int32)
    rate_num = set_ends(jax.random.randint(splits[5], (NSEQ,), 64, RATE_DEN + 1), jax.random.fold_in(splits[5], 1), 64, RATE_DEN).astype(jnp.int32)
    return {"states": states, "head_weight": head_weight, "targets": targets, "positions": positions, "counts": counts, "rate_num": rate_num}


def masked_rows(positions, counts, rate_num):
    seq_count, length = positions.shape
    slot_ids = jnp.arange(CAP, dtype=jnp.int32)
    is_live = slot_ids[None, :] < counts[:, None]
    row_index = (jnp.arange(seq_count, dtype=jnp.int32)[:, None] * length + positions[:, :CAP]).reshape(-1).astype(jnp.int32)
    row_weight = jnp.where(is_live, RATE_DEN / rate_num[:, None].astype(jnp.float32), 0.0).astype(jnp.float32).reshape(-1)
    return row_index, row_weight


def reference(states, head_weight, targets, positions, counts, rate_num):
    row_index, row_weight = masked_rows(positions, counts, rate_num)
    chosen = states[row_index].astype(jnp.float32)
    labels = targets[row_index]
    weight_full = head_weight.astype(jnp.float32)
    logits = jnp.dot(chosen, weight_full, precision=lax.Precision.HIGHEST)
    row_high = jnp.max(logits, axis=1)
    log_total = row_high + jnp.log(jnp.sum(jnp.exp(logits - row_high[:, None]), axis=1))
    target_logit = jnp.take_along_axis(logits, labels[:, None], axis=1)[:, 0]
    mean_loss = jnp.sum(row_weight * (log_total - target_logit)) / (positions.shape[0] * positions.shape[1])
    is_target = jnp.arange(V, dtype=jnp.int32)[None, :] == labels[:, None]
    row_probs = jnp.exp(logits - log_total[:, None])
    grad_logits = (row_weight[:, None] * (row_probs - is_target.astype(jnp.float32))).astype(jnp.bfloat16)
    grad_float = grad_logits.astype(jnp.float32)
    row_grads = jnp.dot(grad_float, weight_full.T, precision=lax.Precision.HIGHEST).astype(jnp.bfloat16)
    grad_hidden = jnp.zeros(states.shape, jnp.bfloat16).at[row_index].set(row_grads)
    grad_weight = jnp.dot(chosen.T, grad_float, precision=lax.Precision.HIGHEST)
    return (mean_loss, grad_hidden, grad_weight)
```

```python
import functools

import jax
import jax.numpy as jnp
from jax import lax
from jax.experimental import pallas as pl
from jax.experimental.pallas import tpu as pltpu
from jax.sharding import PartitionSpec as P

MESH = pl.DeviceIdType.MESH
F32 = jnp.float32
BF16 = jnp.bfloat16

CAP = 48
LIVE = 896
RATE_DEN = 1024
NX = 4
META = 16


def nn(a, b):
    return lax.dot_general(a, b, (((1,), (0,)), ((), ())), preferred_element_type=F32)


def nt(a, b):
    return lax.dot_general(a, b, (((1,), (1,)), ((), ())), preferred_element_type=F32)


def tn(a, b):
    return lax.dot_general(a, b, (((0,), (0,)), ((), ())), preferred_element_type=F32)


def iota(shape, dim):
    return lax.broadcasted_iota(jnp.int32, shape, dim)


def kernel(
    cfg,
    counts_ref,
    rate_ref,
    pos_ref,
    tgt_ref,
    states_ref,
    w_ref,
    loss_ref,
    gh_ref,
    gw_ref,
    s_buf,
    pmt,
    blocks,
    wc,
    xg,
    e_buf,
    xd,
    rank_buf,
    meta,
    qun,
    lse_y,
    lse_x,
    lse_z,
    stat,
    ght,
    red,
    fin,
    u_buf,
    s_sem,
    a_send,
    a_recv,
    w_send,
    w_recv,
    wf_send,
    wf_recv,
    core_send,
    core_recv,
    x_send,
    x_recv,
    zr_send,
    zr_recv,
    e_send,
    e_recv,
    ef_send,
    ef_recv,
    ly_send,
    ly_recv,
    lx_send,
    lx_recv,
    lz_send,
    lz_recv,
    r_send,
    r_recv,
    u_send,
    u_recv,
):
    ny, nx, nz, vw, slots, tokens, seq, all_tokens = cfg
    ndp, nch = 2 * ny, nx * nz
    rc = LIVE // 2
    rh = rc // 2
    width = stat.shape[2]
    dg = 128 // (nch // 2)

    dp = lax.axis_index("dp")
    vo = lax.axis_index("vocab")
    y, c = dp // 2, dp % 2
    x, z = vo // nz, vo % nz
    here = c * ny + y
    piece = z * nx + x
    m, h = piece // 2, piece % 2
    pending = []

    def rem(src, dst, send, recv, device):
        return pltpu.make_async_remote_copy(
            src_ref=src,
            dst_ref=dst,
            send_sem=send,
            recv_sem=recv,
            device_id=device,
            device_id_type=MESH,
        )

    def go(src, dst, send, recv, device):
        copy = rem(src, dst, send, recv, device)
        copy.start()
        pending.append(copy)

    def arrived(dst, send, recv):
        rem(dst, dst, send, recv, (dp, vo)).wait_recv()

    def in_column(yy):
        return (2 * yy + c, vo)

    sibling = (2 * y + 1 - c, vo)
    peer_x = lambda xx: (dp, xx * nz + z)
    peer_z = lambda zz: (dp, x * nz + zz)

    states_copy = pltpu.make_async_copy(
        states_ref.at[:, pl.ds(pl.multiple_of(m * 128, 128), 128)], s_buf, s_sem
    )
    states_copy.start()

    barrier = pltpu.get_barrier_semaphore()
    q = vo
    g, half_q = q // 2, q % 2
    target_vo = 2 * dp + g // (nch // 4)
    src_dp, src_q0 = vo // 2, (nch // 2) * (vo % 2)

    def signal(device):
        pl.semaphore_signal(barrier, inc=1, device_id=device, device_id_type=MESH)

    for k in range(1, ny):
        signal(in_column((y + k) % ny))
    signal(sibling)

    def signal_plane(k, carry):
        signal((dp, (vo + k) % nch))
        return carry

    lax.fori_loop(1, nch, signal_plane, 0)

    def signal_source(t, carry):
        to_self = (src_dp == dp) & (src_q0 + t == vo)

        @pl.when(jnp.logical_not(to_self))
        def _():
            signal((src_dp, src_q0 + t))

        return carry

    lax.fori_loop(0, nch // 2, signal_source, 0)

    lane = iota((8, 128), 1)
    pos0 = jnp.broadcast_to(pos_ref[0:1, 0:128], (8, 128))
    pos1 = jnp.broadcast_to(pos_ref[1:2, 0:128], (8, 128))
    pos1 = pltpu.roll(pos1, CAP, 1)
    tok = jnp.where(lane < CAP, pos0, jnp.where(lane < 2 * CAP, seq + pos1, -1))[0:1]
    pmt[...] = jnp.where(iota((tokens, 128), 0) == tok, 1.0, 0.0).astype(BF16)
    targets = tgt_ref[...]
    row16 = iota((META, tokens), 0)
    parts = jnp.where(
        row16 == 0,
        jnp.right_shift(targets, 8).astype(F32),
        jnp.where(row16 == 1, jnp.bitwise_and(targets, 255).astype(F32), 0.0),
    ).astype(BF16)
    label_rows = nn(parts, pmt[...])
    lane16 = iota((META, 128), 1)
    row16 = iota((META, 128), 0)

    def per_slot(first, second):
        return jnp.where(
            lane16 < CAP, first, jnp.where(lane16 < 2 * CAP, second, 0)
        ).astype(F32)

    r0, r1 = rate_ref[0], rate_ref[1]
    own_meta = jnp.where(row16 == 2, per_slot(jnp.right_shift(r0, 8), jnp.right_shift(r1, 8)), label_rows)
    own_meta = jnp.where(row16 == 3, per_slot(jnp.bitwise_and(r0, 255), jnp.bitwise_and(r1, 255)), own_meta)
    own_meta = jnp.where(row16 == 4, per_slot(counts_ref[0], counts_ref[1]), own_meta)
    states_copy.wait()
    chosen = tn(pmt[...], s_buf[...])
    blocks[c, y, 0:slots, :] = chosen[0:slots].astype(BF16)
    blocks[c, y, slots : slots + META, :] = own_meta.astype(BF16)

    n_to = (ny - 1) + 1 + (nch - 1)
    sends_self = jnp.where(target_vo == vo, 1, 0)
    pl.semaphore_wait(barrier, n_to + ndp - sends_self)

    for k in range(1, ny):
        go(blocks.at[c, y], blocks.at[c, y], a_send.at[k], a_recv.at[k], in_column((y + k) % ny))
    for k in range(1, ny):
        yy = (y + k) % ny
        go(
            w_ref.at[:, pl.ds(pl.multiple_of(yy * vw, vw), vw)],
            wc.at[dp],
            w_send.at[k],
            w_recv.at[k],
            in_column(yy),
        )
    wc[dp] = w_ref[:, pl.ds(pl.multiple_of(y * vw, vw), vw)]
    go(wc.at[dp], wc.at[dp], wf_send.at[0], wf_recv.at[0], sibling)
    for k in range(1, ny):
        arrived(blocks.at[c, (y + ny - k) % ny], a_send.at[k], a_recv.at[k])
    go(blocks.at[c], blocks.at[c], core_send.at[0], core_recv.at[0], sibling)
    arrived(blocks.at[1 - c], core_send.at[0], core_recv.at[0])

    all_meta = blocks[:, :, slots : slots + META, :].astype(F32).reshape(ndp, META, 128)
    count_rows = jnp.sum(
        jnp.where(iota((ndp, META, 128), 1) == 4, all_meta, 0.0), axis=1
    )
    first, second = count_rows[:, 0:1], count_rows[:, CAP : CAP + 1]
    in_all = jnp.broadcast_to(first + second, (ndp, 128)).astype(BF16)

    def order(v):
        return 2 * (v % ny) + v // ny

    earlier = jnp.where(
        order(iota((ndp, ndp), 1)) < order(iota((ndp, ndp), 0)), 1.0, 0.0
    ).astype(BF16)
    offset = nn(earlier, in_all)
    lanes = iota((ndp, 128), 1).astype(F32)
    in_first = lanes < CAP
    place = jnp.where(in_first, lanes, lanes - CAP + first)
    bound = jnp.where(in_first, first, second)
    local_place = jnp.where(in_first, lanes, lanes - CAP)
    live = (local_place < bound) & (lanes < 2 * CAP)
    rank_buf[...] = jnp.where(live, offset + place, -1.0)

    def one_hot(start, rows, a):
        names = iota((rows, 128), 0) + start
        return jnp.where(names.astype(F32) == rank_buf[a : a + 1, :], 1.0, 0.0).astype(BF16)

    acc = jnp.zeros((rh, 128), F32)
    for a in range(ndp):
        pick = one_hot(c * rc + h * rh, rh, a)
        acc += nn(pick[:, 0:slots], blocks[a // ny, a % ny, 0:slots, :])
    xg[piece] = acc.astype(BF16)
    for k in range(1, nx):
        go(xg.at[piece], xg.at[piece], x_send.at[k], x_recv.at[k], peer_x((x + k) % nx))

    def metas(core):
        total = jnp.zeros((rc, META), F32)
        for a in range(ndp):
            total += nt(one_hot(core * rc, rc, a), blocks[a // ny, a % ny, slots : slots + META, :])
        meta[core] = total

    def ring(n, me, block, subs, send, recv, device):
        last = n // 2 - 1

        def moves(step):
            for sub in range(subs):
                for way in (0, 1):
                    if step < last or (sub < subs // 2) == (way == 0):
                        yield way, sub

        def start(step, way, sub):
            origin = (me + n - step) % n if way == 0 else (me + step) % n
            to = (me + 1) % n if way == 0 else (me + n - 1) % n
            ref = block(origin, sub)
            go(ref, ref, send.at[way, step, sub], recv.at[way, step, sub], device(to))

        def wait(step, way, sub):
            origin = (me + n - 1 - step) % n if way == 0 else (me + 1 + step) % n
            ref = block(origin, sub)
            arrived(ref, send.at[way, step, sub], recv.at[way, step, sub])
            return origin

        return last, moves, start, wait

    x_last, x_moves, x_start, x_wait = ring(
        nz, z, lambda o, sub: xg.at[o * nx + sub], nx, zr_send, zr_recv, peer_z
    )

    metas(0)
    for k in range(1, nx):
        arrived(xg.at[z * nx + (x + nx - k) % nx], x_send.at[k], x_recv.at[k])
    for way, sub in x_moves(0):
        x_start(0, way, sub)

    metas(1)
    for a in range(ndp):
        qun[:, a * 128 : (a + 1) * 128] = one_hot(half_q * rc, rc, a)

    def w_arrive(k):
        from_dp = 2 * ((y + ny - k) % ny) + c
        arrived(wc.at[from_dp], w_send.at[k], w_recv.at[k])
        go(wc.at[from_dp], wc.at[from_dp], wf_send.at[k], wf_recv.at[k], sibling)

    w_order = sorted(range(1, ny), key=lambda k: min(k, ny - k))
    for step in range(x_last + 1):
        following = set(x_moves(step + 1)) if step < x_last else set()
        for way, sub in x_moves(step):
            x_wait(step, way, sub)
            if (way, sub) in following:
                x_start(step + 1, way, sub)
        take = len(w_order) if step == x_last else 2
        for k in w_order[:take]:
            w_arrive(k)
        w_order = w_order[take:]
    for k in range(ny):
        from_dp = 2 * ((y + ny - k) % ny) + 1 - c
        arrived(wc.at[from_dp], wf_send.at[k], wf_recv.at[k])

    logits = jnp.zeros((rc, vw), F32)
    for mm in range(ndp):
        rows = xg[2 * mm : 2 * mm + 2].reshape(rc, 128)
        logits += nn(rows, wc[mm])
    high = jnp.max(logits, axis=1, keepdims=True)
    powers = jnp.exp(logits - high)
    sums = jnp.sum(powers, axis=1, keepdims=True)
    lse = high + jnp.log(sums)
    own_part = powers * (1.0 / sums)
    for sub in range(2):
        e_buf[c, y, sub] = own_part[sub * rh : (sub + 1) * rh].astype(BF16)

    def label_of(core):
        rows = meta[core]
        return (rows[:, 0:1] * 256.0 + rows[:, 1:2]).astype(jnp.int32)

    def weight_of(core):
        rows = meta[core]
        return RATE_DEN / (rows[:, 2:3] * 256.0 + rows[:, 3:4])

    labels, weights = label_of(c), weight_of(c)
    hit = iota((rc, vw), 1) == labels - (vo * (vw * ny) + y * vw)
    of_targets = jnp.sum(jnp.sum(jnp.where(hit, logits * weights, 0.0), axis=1, keepdims=True), axis=0, keepdims=True)

    lse_row = jnp.transpose(jnp.broadcast_to(lse, (rc, 128)))[0:1]
    lse_y[y, :, 0:rc] = lse_row
    lse_y[y, :, rc:width] = jnp.broadcast_to(of_targets, (1, width - rc))

    for k in range(1, ny):
        go(lse_y.at[y], lse_y.at[y], ly_send.at[k], ly_recv.at[k], in_column((y + k) % ny))

    e_last, e_moves, e_start, e_wait = ring(
        ny, y, lambda o, sub: e_buf.at[c, o, sub], 2, e_send, e_recv, in_column
    )
    for way, sub in e_moves(0):
        e_start(0, way, sub)

    def share(offset, sub):
        o = (y + offset) % ny
        ref = e_buf.at[c, o, sub]
        go(ref, ref, ef_send.at[offset, sub], ef_recv.at[offset, sub], sibling)

    def shared(offset, sub):
        o = (y + offset) % ny
        arrived(e_buf.at[1 - c, o, sub], ef_send.at[offset, sub], ef_recv.at[offset, sub])

    share(0, 0)
    share(0, 1)
    go(xg.at[pl.ds(2 * (dp + 1 - 2 * c), 2)], xd.at[c], core_send.at[1], core_recv.at[1], sibling)
    xd[c] = xg[pl.ds(2 * dp, 2)]

    in_rows = iota((1, width), 1) < rc

    def combine(ref, n):
        rows = [ref[i] for i in range(n)]
        top = functools.reduce(jnp.maximum, rows)
        exps = functools.reduce(jnp.add, [jnp.exp(r - top) for r in rows])
        plain = functools.reduce(jnp.add, rows)
        return jnp.where(in_rows, top + jnp.log(exps), plain)

    for k in range(1, ny):
        arrived(lse_y.at[(y + ny - k) % ny], ly_send.at[k], ly_recv.at[k])
    lse_x[x] = combine(lse_y, ny)
    for k in range(1, nx):
        go(lse_x.at[x], lse_x.at[x], lx_send.at[k], lx_recv.at[k], peer_x((x + k) % nx))
    for k in range(1, nx):
        arrived(lse_x.at[(x + nx - k) % nx], lx_send.at[k], lx_recv.at[k])
    lse_z[z] = combine(lse_x, nx)
    for k in range(1, nz):
        go(lse_z.at[z], lse_z.at[z], lz_send.at[k], lz_recv.at[k], peer_z((z + k) % nz))
    for k in range(1, nz):
        arrived(lse_z.at[(z + nz - k) % nz], lz_send.at[k], lz_recv.at[k])
    log_total = combine(lse_z, nz)
    for k in range(ny):
        stat[c, k : k + 1, :] = lse_y[(y + k) % ny]
    stat[c, ny : ny + 1, :] = log_total
    go(stat.at[c], stat.at[c], core_send.at[2], core_recv.at[2], sibling)

    arrived(xd.at[1 - c], core_send.at[1], core_recv.at[1])
    features = [jnp.transpose(xd[core].reshape(rc, 128)) for core in range(2)]
    arrived(stat.at[1 - c], core_send.at[2], core_recv.at[2])

    scales, label_cols, weight_cols = [], [], []
    loss = jnp.zeros((1, 1), F32)
    for core in range(2):
        rows = stat[core]
        cols = jnp.transpose(rows)[0:rc]
        label_cols.append(label_of(core))
        weight_cols.append(weight_of(core))
        total_col = cols[:, ny : ny + 1]
        scales.append(weight_cols[core] * jnp.exp(cols - total_col))
        loss += jnp.sum(weight_cols[core] * total_col, axis=0, keepdims=True)
        loss -= rows[ny : ny + 1, rc : rc + 1]
    loss_ref[...] = loss * (1.0 / all_tokens)

    def process(offset, fresh):
        o = (y + offset) % ny
        columns = pl.ds(pl.multiple_of(o * vw, vw), vw)
        grad = jnp.zeros((128, vw), F32)
        for core in range(2):
            part = e_buf[core, o].reshape(rc, vw).astype(F32)
            hit = iota((rc, vw), 1) == label_cols[core] - (vo * (vw * ny) + o * vw)
            scaled = part * scales[core][:, offset : offset + 1]
            g_logits = jnp.where(hit, scaled - weight_cols[core], scaled).astype(BF16)
            grad += nn(features[core], g_logits)
            term = nt(w_ref[:, columns], g_logits)
            if fresh:
                ght[core] = term
            else:
                ght[core] += term
        gw_ref[:, columns] = grad

    shared(0, 0)
    shared(0, 1)
    process(0, True)
    for step in range(e_last + 1):
        following = set(e_moves(step + 1)) if step < e_last else set()
        came = set()
        for way, sub in e_moves(step):
            e_wait(step, way, sub)
            if (way, sub) in following:
                e_start(step + 1, way, sub)
            offset = (ny - 1 - step) if way == 0 else 1 + step
            share(offset, sub)
            came.add(offset)
        for offset in sorted(came):
            shared(offset, 0)
            shared(offset, 1)
            process(offset, False)

    def piece_of(qq):
        return ght.at[qq % 2, pl.ds(pl.multiple_of((qq // 2) * dg, dg), dg), :]

    def send_piece(k, carry):
        to = (vo + k) % nch
        rem(piece_of(to), red.at[vo], r_send.at[k], r_recv.at[k], (dp, to)).start()
        return carry

    lax.fori_loop(1, nch, send_piece, 0)
    red[vo] = ght[half_q, pl.ds(pl.multiple_of(g * dg, dg), dg), :]

    def take_piece(k, carry):
        frm = (vo + nch - k) % nch
        arrived(red.at[frm], r_send.at[k], r_recv.at[k])
        return carry

    lax.fori_loop(1, nch, take_piece, 0)
    final = jnp.sum(red[...], axis=0)
    in_slots = nn(final.astype(BF16), qun[...])
    for a in range(ndp):
        fin[a] = in_slots[:, a * 128 : (a + 1) * 128]
    slot = vo % (nch // 2)

    def is_self(a):
        return (target_vo == vo) & (a == here)

    def send_final(a, carry):
        to = (2 * (a % ny) + a // ny, target_vo)

        @pl.when(jnp.logical_not(is_self(a)))
        def _():
            rem(fin.at[a], u_buf.at[slot], u_send.at[a], u_recv.at[slot], to).start()

        return carry

    lax.fori_loop(0, ndp, send_final, 0)

    @pl.when(target_vo == vo)
    def _():
        u_buf[slot] = fin[here]

    def take_final(t, carry):
        from_self = (src_dp == dp) & (src_q0 + t == vo)

        @pl.when(jnp.logical_not(from_self))
        def _():
            arrived(u_buf.at[t], u_send.at[0], u_recv.at[t])

        return carry

    lax.fori_loop(0, nch // 2, take_final, 0)
    pieces = [u_buf[2 * t] + u_buf[2 * t + 1] for t in range(nch // 4)]
    columns = jnp.concatenate(pieces, axis=0).astype(BF16)
    gh_ref[...] = nt(pmt[...], columns).astype(BF16)

    for copy in pending:
        copy.wait_send()

    def sent_piece(k, carry):
        to = (vo + k) % nch
        rem(piece_of(to), red.at[vo], r_send.at[k], r_recv.at[k], (dp, to)).wait_send()
        return carry

    lax.fori_loop(1, nch, sent_piece, 0)

    def sent_final(a, carry):
        to = (2 * (a % ny) + a // ny, target_vo)

        @pl.when(jnp.logical_not(is_self(a)))
        def _():
            rem(fin.at[a], u_buf.at[slot], u_send.at[a], u_recv.at[slot], to).wait_send()

        return carry

    lax.fori_loop(0, ndp, sent_final, 0)


def local(states, head_weight, targets, positions, counts, rate_num):
    ndp = lax.axis_size("dp")
    nch = lax.axis_size("vocab")
    ny, nx, nz = ndp // 2, NX, nch // NX
    tokens, d = states.shape
    vw = head_weight.shape[1] // ny
    seqs, seq = positions.shape
    slots = seqs * CAP
    rc = LIVE // 2
    width = -(-(rc + 1) // 128) * 128
    dg = 128 // (nch // 2)
    stat_rows = -(-(ny + 1) // 8) * 8
    cfg = (ny, nx, nz, vw, slots, tokens, seq, ndp * tokens)
    dma = pltpu.SemaphoreType.DMA
    scratch = [
        pltpu.VMEM((tokens, 128), BF16),
        pltpu.VMEM((tokens, 128), BF16),
        pltpu.VMEM((2, ny, slots + META, 128), BF16),
        pltpu.VMEM((ndp, 128, vw), BF16),
        pltpu.VMEM((nch, rc // 2, 128), BF16),
        pltpu.VMEM((2, ny, 2, rc // 2, vw), BF16),
        pltpu.VMEM((2, 2, rc // 2, 128), BF16),
        pltpu.VMEM((ndp, 128), F32),
        pltpu.VMEM((2, rc, META), F32),
        pltpu.VMEM((rc, ndp * 128), BF16),
        pltpu.VMEM((ny, 1, width), F32),
        pltpu.VMEM((nx, 1, width), F32),
        pltpu.VMEM((nz, 1, width), F32),
        pltpu.VMEM((2, stat_rows, width), F32),
        pltpu.VMEM((2, 128, rc), F32),
        pltpu.VMEM((nch, dg, rc), F32),
        pltpu.VMEM((ndp, dg, 128), F32),
        pltpu.VMEM((nch // 2, dg, 128), F32),
        dma,
        dma((ny,)),
        dma((ny,)),
        dma((ny,)),
        dma((ny,)),
        dma((ny,)),
        dma((ny,)),
        dma((3,)),
        dma((3,)),
        dma((nx,)),
        dma((nx,)),
        dma((2, nz // 2, nx)),
        dma((2, nz // 2, nx)),
        dma((2, ny // 2, 2)),
        dma((2, ny // 2, 2)),
        dma((ny, 2)),
        dma((ny, 2)),
        dma((ny,)),
        dma((ny,)),
        dma((nx,)),
        dma((nx,)),
        dma((nz,)),
        dma((nz,)),
        dma((nch,)),
        dma((nch,)),
        dma((ndp,)),
        dma((nch // 2,)),
    ]
    vmem = pl.BlockSpec(memory_space=pltpu.VMEM)
    smem = pl.BlockSpec(memory_space=pltpu.SMEM)
    loss, grad_hidden, grad_weight = pl.pallas_call(
        functools.partial(kernel, cfg),
        out_shape=(
            jax.ShapeDtypeStruct((1, 1), F32),
            jax.ShapeDtypeStruct((tokens, d // nch), BF16),
            jax.ShapeDtypeStruct(head_weight.shape, F32),
        ),
        in_specs=[smem, smem, vmem, vmem, pl.BlockSpec(memory_space=pl.ANY), vmem],
        out_specs=(vmem, vmem, vmem),
        scratch_shapes=scratch,
        compiler_params=pltpu.CompilerParams(
            collective_id=0, has_side_effects=True, vmem_limit_bytes=48 * 1024 * 1024
        ),
    )(counts, rate_num, positions, targets.reshape(1, tokens), states, head_weight)
    return loss[0, 0], grad_hidden, grad_weight


def solution(mesh):
    return jax.shard_map(
        local,
        mesh=mesh,
        in_specs=(P("dp", None), P("dp", "vocab"), P("dp"), P("dp", None), P("dp"), P("dp")),
        out_specs=(P(), P("dp", "vocab"), P("dp", "vocab")),
        check_vma=False,
    )
```

```python
import functools

import jax
import jax.numpy as jnp
from jax import lax
from jax.experimental import pallas as pl
from jax.experimental.pallas import tpu as pltpu
from jax.sharding import PartitionSpec as P

MESH = pl.DeviceIdType.MESH
F32 = jnp.float32
BF16 = jnp.bfloat16

CAP = 48
LIVE = 896
RATE_DEN = 1024
NX = 4
META = 16


def nn(a, b):
    return lax.dot_general(a, b, (((1,), (0,)), ((), ())), preferred_element_type=F32)


def nt(a, b):
    return lax.dot_general(a, b, (((1,), (1,)), ((), ())), preferred_element_type=F32)


def tn(a, b):
    return lax.dot_general(a, b, (((0,), (0,)), ((), ())), preferred_element_type=F32)


def iota(shape, dim):
    return lax.broadcasted_iota(jnp.int32, shape, dim)


def kernel(
    cfg,
    counts_hbm,
    rate_hbm,
    pos_hbm,
    tgt_hbm,
    states_hbm,
    w_hbm,
    loss_ref,
    gh_ref,
    gw_hbm,
    counts_ref,
    rate_ref,
    pos_ref,
    tgt_ref,
    w_ref,
    s_buf,
    pmt,
    blocks,
    wc,
    xg,
    e_buf,
    g_buf,
    xd,
    rank_buf,
    meta,
    qun,
    lse_y,
    lse_xz,
    loss_buf,
    gw_ref,
    ght,
    red,
    fin,
    u_buf,
    in_sem,
    a_sem,
    w_send,
    w_recv,
    wf_sem,
    core_send,
    core_recv,
    x_sem,
    zr_send,
    zr_recv,
    zu_send,
    zu_recv,
    xf_sem,
    e_send,
    e_recv,
    g_send,
    g_recv,
    ly_sem,
    lp_sem,
    r_send,
    r_recv,
    u_sem,
    out_sem,
):
    ny, nx, nz, vw, slots, tokens, seq, all_tokens = cfg
    ndp, nch = 2 * ny, nx * nz
    rg = LIVE // 4
    rp = rg // 2
    width = lse_y.shape[3]
    dg = 256 // nch

    dp = lax.axis_index("dp")
    vo = lax.axis_index("vocab")
    y, c = dp // 2, dp % 2
    x, z = vo // nz, vo % nz
    here = c * ny + y
    piece = z * nx + x
    m, h = piece // 2, piece % 2

    def rem(src, dst, send, recv, device):
        return pltpu.make_async_remote_copy(
            src_ref=src,
            dst_ref=dst,
            send_sem=send,
            recv_sem=recv,
            device_id=device,
            device_id_type=MESH,
        )

    def go(src, dst, send, recv, device):
        rem(src, dst, send, recv, device).start()

    def arrived(dst, recv):
        rem(dst, dst, recv, recv, (dp, vo)).wait_recv()

    def gone(src, send):
        rem(src, src, send, send, (dp, vo)).wait_send()

    def in_column(yy):
        return (2 * yy + c, vo)

    sibling = (2 * y + 1 - c, vo)
    peer_x = lambda xx: (dp, xx * nz + z)
    peer_z = lambda zz: (dp, x * nz + zz)

    states_slice = states_hbm.at[:, pl.ds(pl.multiple_of(m * 128, 128), 128)]
    loads = [
        pltpu.make_async_copy(src, dst, in_sem.at[i])
        for i, (src, dst) in enumerate(
            [
                (pos_hbm, pos_ref),
                (tgt_hbm, tgt_ref),
                (counts_hbm, counts_ref),
                (rate_hbm, rate_ref),
                (states_slice, s_buf),
                (w_hbm, w_ref.at[c]),
            ]
        )
    ]
    for load in loads:
        load.start()

    barrier = pltpu.get_barrier_semaphore()
    q = vo
    target_vo = 4 * y + q // (nch // 4)
    src_y, src_q0 = vo // 4, (nch // 4) * (vo % 4)
    to_self = target_vo == vo

    def signal(device):
        pl.semaphore_signal(barrier, inc=1, device_id=device, device_id_type=MESH)

    for k in range(1, ny):
        signal(in_column((y + k) % ny))
    signal(sibling)

    def signal_plane(k, carry):
        signal((dp, (vo + k) % nch))
        return carry

    lax.fori_loop(1, nch, signal_plane, 0)

    def signal_source(t, carry):
        source = (2 * src_y + t // (nch // 4), src_q0 + t % (nch // 4))

        @pl.when(jnp.logical_not((source[0] == dp) & (source[1] == vo)))
        def _():
            signal(source)

        return carry

    lax.fori_loop(0, nch // 2, signal_source, 0)

    loads[0].wait()
    lane = iota((8, 128), 1)
    pos0 = jnp.broadcast_to(pos_ref[0:1, 0:128], (8, 128))
    pos1 = jnp.broadcast_to(pos_ref[1:2, 0:128], (8, 128))
    pos1 = pltpu.roll(pos1, CAP, 1)
    tok = jnp.where(lane < CAP, pos0, jnp.where(lane < 2 * CAP, seq + pos1, -1))[0:1]
    pmt[...] = jnp.where(iota((tokens, 128), 0) == tok, 1.0, 0.0).astype(BF16)
    loads[1].wait()
    targets = tgt_ref[...]
    row16 = iota((META, tokens), 0)
    parts = jnp.where(
        row16 == 0,
        jnp.right_shift(targets, 8).astype(F32),
        jnp.where(row16 == 1, jnp.bitwise_and(targets, 255).astype(F32), 0.0),
    ).astype(BF16)
    label_rows = nn(parts, pmt[...])
    lane16 = iota((META, 128), 1)
    row16 = iota((META, 128), 0)

    def per_slot(first, second):
        return jnp.where(
            lane16 < CAP, first, jnp.where(lane16 < 2 * CAP, second, 0)
        ).astype(F32)

    loads[2].wait()
    loads[3].wait()
    r0, r1 = rate_ref[0], rate_ref[1]
    own_meta = jnp.where(
        row16 == 2, per_slot(jnp.right_shift(r0, 8), jnp.right_shift(r1, 8)), label_rows
    )
    own_meta = jnp.where(
        row16 == 3, per_slot(jnp.bitwise_and(r0, 255), jnp.bitwise_and(r1, 255)), own_meta
    )
    own_meta = jnp.where(row16 == 4, per_slot(counts_ref[0], counts_ref[1]), own_meta)
    loads[4].wait()
    chosen = tn(pmt[...], s_buf[...])
    blocks[c, y, 0:slots, :] = chosen[0:slots].astype(BF16)
    blocks[c, y, slots : slots + META, :] = own_meta.astype(BF16)

    n_to = (ny - 1) + 1 + (nch - 1)
    pl.semaphore_wait(barrier, n_to + ndp - jnp.where(to_self, 1, 0))

    for k in range(1, ny):
        go(blocks.at[c, y], blocks.at[c, y], a_sem.at[0], a_sem.at[1], in_column((y + k) % ny))
    loads[5].wait()

    def own_columns(o):
        return w_ref.at[c, :, pl.ds(pl.multiple_of(o * vw, vw), vw)]

    near = sorted(range(1, ny), key=lambda k: min(k, ny - k))
    for k in reversed(near):
        yy = (y + k) % ny
        go(own_columns(yy), wc.at[dp], w_send, w_recv.at[k], in_column(yy))
    wc[dp] = own_columns(y)[...]
    go(wc.at[dp], wc.at[dp], wf_sem.at[0], wf_sem.at[1], sibling)
    go(w_ref.at[c], w_ref.at[c], core_send.at[1], core_recv.at[1], sibling)
    arrived(blocks.at[c, 0 : ny - 1], a_sem.at[1])
    go(blocks.at[c], blocks.at[c], core_send.at[0], core_recv.at[0], sibling)
    arrived(blocks.at[1 - c], core_recv.at[0])

    all_meta = blocks[:, :, slots : slots + META, :].astype(F32).reshape(ndp, META, 128)
    count_rows = jnp.sum(
        jnp.where(iota((ndp, META, 128), 1) == 4, all_meta, 0.0), axis=1
    )
    first, second = count_rows[:, 0:1], count_rows[:, CAP : CAP + 1]
    in_all = jnp.broadcast_to(first + second, (ndp, 128)).astype(BF16)

    def order(v):
        return 2 * (v % ny) + v // ny

    earlier = jnp.where(
        order(iota((ndp, ndp), 1)) < order(iota((ndp, ndp), 0)), 1.0, 0.0
    ).astype(BF16)
    offset = nn(earlier, in_all)
    lanes = iota((ndp, 128), 1).astype(F32)
    in_first = lanes < CAP
    place = jnp.where(in_first, lanes, lanes - CAP + first)
    bound = jnp.where(in_first, first, second)
    local_place = jnp.where(in_first, lanes, lanes - CAP)
    live = (local_place < bound) & (lanes < 2 * CAP)
    rank_buf[...] = jnp.where(live, offset + place, -1.0)

    def one_hot(start, rows, a):
        names = iota((rows, 128), 0) + start
        return jnp.where(names.astype(F32) == rank_buf[a : a + 1, :], 1.0, 0.0).astype(BF16)

    for t in range(2):
        acc = jnp.zeros((rp, 128), F32)
        for a in range(ndp):
            pick = one_hot((2 * c + t) * rg + h * rp, rp, a)
            acc += nn(pick[:, 0:slots], blocks[a // ny, a % ny, 0:slots, :])
        xg[t, piece] = acc.astype(BF16)
        own = xg.at[t, piece]
        if t == 0:
            for k in range(1, nx):
                go(own, own, x_sem.at[0], x_sem.at[1], peer_x((x + k) % nx))
        else:
            for k in sorted(range(1, nz), key=lambda k: min(k, nz - k)):
                go(own, own, zu_send, zu_recv.at[k], peer_z((z + k) % nz))
            for k in range(1, nx):
                go(own, own, xf_sem.at[0], xf_sem.at[1], peer_x((x + k) % nx))

    def metas(t):
        total = jnp.zeros((rg, META), F32)
        for a in range(ndp):
            pick = one_hot((2 * c + t) * rg, rg, a)
            qun[t, :, a * 128 : (a + 1) * 128] = pick
            total += nt(pick, blocks[a // ny, a % ny, slots : slots + META, :])
        meta[t] = total

    def ring(n, me, block, subs, send, recv, device):
        last = n // 2 - 1

        def moves(step):
            for sub in range(subs):
                for way in (0, 1):
                    if step < last or (sub < subs // 2) == (way == 0):
                        yield way, sub

        def start(step):
            for way, sub in moves(step):
                start_one(step, way, sub)

        def start_one(step, way, sub):
            origin = (me + n - step) % n if way == 0 else (me + step) % n
            to = (me + 1) % n if way == 0 else (me + n - 1) % n
            ref = block(origin, sub)
            go(ref, ref, send, recv.at[way, step, sub], device(to))

        def advance(step, then=None):
            following = set(moves(step + 1)) if step < last else set()
            for way, sub in moves(step):
                origin = (me + n - 1 - step) % n if way == 0 else (me + 1 + step) % n
                ref = block(origin, sub)
                arrived(ref, recv.at[way, step, sub])
                if (way, sub) in following:
                    start_one(step + 1, way, sub)
                if then is not None:
                    then((n - 1 - step) if way == 0 else 1 + step, sub)

        return last, start, advance

    half_x = nx // 2
    x_last, x_start, x_advance = ring(
        nz,
        z,
        lambda o, sub: xg.at[0, pl.ds(o * nx + sub * half_x, half_x)],
        2,
        zr_send,
        zr_recv,
        peer_z,
    )

    def pass_on(k):
        ref = xg.at[1, ((z + nz - k) % nz) * nx + x]
        arrived(ref, zu_recv.at[k])
        for i in range(1, nx):
            go(ref, ref, xf_sem.at[0], xf_sem.at[1], peer_x((x + i) % nx))

    def w_arrive(k):
        ref = wc.at[2 * ((y + ny - k) % ny) + c]
        arrived(ref, w_recv.at[k])
        go(ref, ref, wf_sem.at[0], wf_sem.at[1], sibling)

    z_near = sorted(range(1, nz), key=lambda k: min(k, nz - k))
    w_near = list(near)
    arrived(xg.at[0, 0 : nx - 1], x_sem.at[1])
    x_start(0)
    for k in z_near[:2]:
        pass_on(k)
    z_near = z_near[2:]
    metas(0)
    for step in range(x_last + 1):
        x_advance(step)
        take = 2 if step < x_last else len(z_near)
        for k in z_near[:take]:
            pass_on(k)
        z_near = z_near[take:]
        if step == 0:
            metas(1)
        take = 2 if step < x_last else len(w_near)
        for k in w_near[:take]:
            w_arrive(k)
        w_near = w_near[take:]
    arrived(wc.at[0:ny], wf_sem.at[1])

    def label_of(t):
        rows = meta[t]
        return (rows[:, 0:1] * 256.0 + rows[:, 1:2]).astype(jnp.int32)

    def weight_of(t):
        rows = meta[t]
        return RATE_DEN / (rows[:, 2:3] * 256.0 + rows[:, 3:4])

    e_rings = [
        ring(
            ny,
            y,
            lambda o, sub, t=t: e_buf.at[t, o, sub],
            2,
            e_send.at[t],
            e_recv.at[t],
            in_column,
        )
        for t in range(2)
    ]
    e_last = e_rings[0][0]

    def softmax_part(t):
        logits = jnp.zeros((rg, vw), F32)
        for mm in range(0, ndp, 2):
            rows = [xg[t, 2 * (mm + i) : 2 * (mm + i) + 2].reshape(rg, 128) for i in range(2)]
            logits += nn(
                jnp.concatenate(rows, axis=1), wc[mm : mm + 2].reshape(256, vw)
            )
        high = jnp.max(logits, axis=1, keepdims=True)
        powers = jnp.exp(logits - high)
        sums = jnp.sum(powers, axis=1, keepdims=True)
        lse = high + jnp.log(sums)
        own_part = powers * (1.0 / sums)
        for sub in range(2):
            e_buf[t, y, sub] = own_part[sub * rp : (sub + 1) * rp].astype(BF16)
        hit = iota((rg, vw), 1) == label_of(t) - (vo * (vw * ny) + y * vw)
        of_targets = jnp.sum(
            jnp.sum(jnp.where(hit, logits * weight_of(t), 0.0), axis=1, keepdims=True),
            axis=0,
            keepdims=True,
        )
        lse_row = jnp.transpose(jnp.broadcast_to(lse, (rg, 128)))[0:1]
        lse_y[y, t, :, 0:rg] = lse_row
        lse_y[y, t, :, rg:width] = jnp.broadcast_to(of_targets, (1, width - rg))
        go(
            xg.at[t, pl.ds(2 * (dp + 1 - 2 * c), 2)],
            xd.at[c, t],
            core_send.at[2 + t],
            core_recv.at[2 + t],
            sibling,
        )
        xd[c, t] = xg[t, pl.ds(2 * dp, 2)]

    in_rows = iota((1, width), 1) < rg

    def combine(rows):
        top = functools.reduce(jnp.maximum, rows)
        exps = functools.reduce(jnp.add, [jnp.exp(r - top) for r in rows])
        plain = functools.reduce(jnp.add, rows)
        return jnp.where(in_rows, top + jnp.log(exps), plain)

    def send_stats():
        for k in range(1, ny):
            go(lse_y.at[y], lse_y.at[y], ly_sem.at[0], ly_sem.at[1], in_column((y + k) % ny))

    def column_stats():
        arrived(lse_y.at[0 : ny - 1], ly_sem.at[1])
        for t in range(2):
            lse_xz[vo, t] = combine([lse_y[i, t] for i in range(ny)])

        def send(k, carry):
            go(lse_xz.at[vo], lse_xz.at[vo], lp_sem.at[0], lp_sem.at[1], (dp, (vo + k) % nch))
            return carry

        lax.fori_loop(1, nch, send, 0)

    features, scales, labels, weights = {}, {}, {}, {}

    def plane_stats():
        arrived(lse_xz.at[0 : nch - 1], lp_sem.at[1])
        loss = jnp.zeros((1, 1), F32)
        for t in range(2):
            log_total = combine([lse_xz[i, t] for i in range(nch)])
            rows = [lse_y[(y + k) % ny, t] for k in range(ny)] + [log_total]
            rows += [jnp.zeros_like(log_total)] * (-len(rows) % 8)
            cols = jnp.transpose(jnp.concatenate(rows, axis=0))[0:rg]
            labels[t], weights[t] = label_of(t), weight_of(t)
            total_col = cols[:, ny : ny + 1]
            scales[t] = weights[t] * jnp.exp(cols - total_col)
            loss += jnp.sum(weights[t] * total_col, axis=0, keepdims=True)
            loss -= log_total[:, rg : rg + 1]
        loss_buf[c] = jnp.broadcast_to(loss, loss_buf.shape[1:])
        go(loss_buf.at[c], loss_buf.at[c], core_send.at[4], core_recv.at[4], sibling)
        arrived(w_ref.at[1 - c], core_recv.at[1])
        for t in range(2):
            features[t] = jnp.transpose(xd[c, t].reshape(rg, 128))

    def own(t, offset):
        o = (y + offset) % ny
        columns = pl.ds(pl.multiple_of(o * vw, vw), vw)
        part = e_buf[t, o].reshape(rg, vw).astype(F32)
        hit = iota((rg, vw), 1) == labels[t] - (vo * (vw * ny) + o * vw)
        scaled = part * scales[t][:, offset : offset + 1]
        g_logits = jnp.where(hit, scaled - weights[t], scaled).astype(BF16)
        g_buf[c, t, o] = g_logits
        go(g_buf.at[c, t, o], g_buf.at[c, t, o], g_send, g_recv.at[t, offset], sibling)
        term = nt(w_ref[:, :, columns].reshape(256, vw), g_logits)
        if offset == 0:
            ght[t] = term
        else:
            ght[t] += term
        grad = nn(features[t], g_logits)
        if t == 0:
            gw_ref[:, columns] = grad
        else:
            gw_ref[:, columns] += grad

    def others():
        for t in range(2):
            arrived(xd.at[1 - c, t], core_recv.at[2 + t])
        turned = [jnp.transpose(xd[1 - c, t].reshape(rg, 128)) for t in range(2)]
        for offset in range(ny):
            o = (y + offset) % ny
            columns = pl.ds(pl.multiple_of(o * vw, vw), vw)
            grad = gw_ref[:, columns]
            for t in range(2):
                arrived(g_buf.at[1 - c, t, o], g_recv.at[t, offset])
                grad += nn(turned[t], g_buf[1 - c, t, o])
            gw_ref[:, columns] = grad

    def piece_of(t, qq):
        return ght.at[t, pl.ds(pl.multiple_of(qq * dg, dg), dg), :]

    def send_pieces(t):
        def send(k, carry):
            to = (vo + k) % nch
            go(piece_of(t, to), red.at[t, vo], r_send, r_recv.at[t], (dp, to))
            return carry

        lax.fori_loop(1, nch, send, 0)
        red[t, vo] = piece_of(t, vo)[...]

    def add_pieces(t):
        arrived(red.at[t, 0 : nch - 1], r_recv.at[t])
        return nn(jnp.sum(red[t], axis=0).astype(BF16), qun[t])

    softmax_part(0)
    e_rings[0][1](0)
    arrived(xg.at[1, 0 : (nx - 1) * nz], xf_sem.at[1])
    softmax_part(1)
    send_stats()
    e_rings[1][1](0)
    arrival = [sorted({ny - 1 - s, 1 + s}) for s in range(e_last + 1)]
    ready = {0: [0], 1: [0]}

    def spread(t, step):
        e_rings[t][2](step)
        ready[t] += arrival[step]

    def work(t, count):
        for _ in range(min(count, len(ready[t]))):
            offset = ready[t].pop(0)
            own(t, offset)
            if offset == ny // 2:
                send_pieces(t)

    spread(0, 0)
    column_stats()
    spread(1, 0)
    if e_last > 0:
        spread(0, 1)
    plane_stats()
    for step in range(1, e_last + 1):
        spread(1, step)
        work(0, 4)
        if step < e_last:
            spread(0, step + 1)
            work(0, 2)
            work(1, 1)
    work(0, ny)
    work(1, ny)
    others()
    gw_copy = pltpu.make_async_copy(gw_ref, gw_hbm, out_sem)
    gw_copy.start()
    arrived(loss_buf.at[1 - c], core_recv.at[4])
    loss_ref[...] = (loss_buf[0, :, 0:1] + loss_buf[1, :, 0:1]) * (1.0 / all_tokens)
    in_slots = add_pieces(0)
    in_slots += add_pieces(1)
    for a in range(ndp):
        fin[a] = in_slots[:, a * 128 : (a + 1) * 128]
    slot = c * (nch // 4) + q % (nch // 4)

    def send_final(a, carry):
        @pl.when(jnp.logical_not(to_self & (a == here)))
        def _():
            to = (2 * (a % ny) + a // ny, target_vo)
            go(fin.at[a], u_buf.at[slot], u_sem.at[0], u_sem.at[1], to)

        return carry

    lax.fori_loop(0, ndp, send_final, 0)

    @pl.when(to_self)
    def _():
        u_buf[slot] = fin[here]

    gone(blocks.at[c, 0 : ny - 1], a_sem.at[0])
    gone(wc.at[0 : ny - 1], w_send)
    gone(wc.at[0:ny], wf_sem.at[0])
    gone(blocks.at[c], core_send.at[0])
    gone(w_ref.at[c], core_send.at[1])
    for t in range(2):
        gone(xd.at[c, t], core_send.at[2 + t])
        gone(e_buf.at[t, 0 : ny - 1], e_send.at[t])
    gone(loss_buf.at[c], core_send.at[4])
    gone(xg.at[0, 0 : nx - 1], x_sem.at[0])
    gone(xg.at[0, 0 : (nz - 1) * nx], zr_send)
    gone(xg.at[1, 0 : nz - 1], zu_send)
    gone(xg.at[1, 0 : (nx - 1) * nz], xf_sem.at[0])
    gone(lse_y.at[0 : ny - 1], ly_sem.at[0])
    gone(lse_xz.at[0 : nch - 1], lp_sem.at[0])
    gone(g_buf.at[c], g_send)
    gone(red.at[:, 0 : nch - 1], r_send)
    gw_copy.wait()

    @pl.when(to_self)
    def _():
        arrived(u_buf.at[0 : nch // 2 - 1], u_sem.at[1])
        gone(fin.at[0 : ndp - 1], u_sem.at[0])

    @pl.when(jnp.logical_not(to_self))
    def _():
        arrived(u_buf, u_sem.at[1])
        gone(fin, u_sem.at[0])

    half = nch // 4
    pieces = [u_buf[t] + u_buf[half + t] for t in range(half)]
    columns = jnp.concatenate(pieces, axis=0).astype(BF16)
    gh_ref[...] = nt(columns, pmt[...]).astype(BF16)


def copies(loss, gh, gw, loss_out, gh_out, gw_out, loss_buf, gh_buf, gw_buf, sems):
    rows = gw.shape[0] // 4
    moves = [(loss, loss_buf, loss_out), (gh, gh_buf, gh_out)]
    moves += [tuple(r.at[pl.ds(k * rows, rows)] for r in (gw, gw_buf, gw_out)) for k in range(4)]
    into = [pltpu.make_async_copy(a, b, sems.at[0, k]) for k, (a, b, _) in enumerate(moves)]
    out = [pltpu.make_async_copy(b, d, sems.at[1, k]) for k, (_, b, d) in enumerate(moves)]
    for move in into:
        move.start()
    for first, then in zip(into, out):
        first.wait()
        then.start()
    for move in out:
        move.wait()


def local(states, head_weight, targets, positions, counts, rate_num):
    ndp = lax.axis_size("dp")
    nch = lax.axis_size("vocab")
    ny, nx, nz = ndp // 2, NX, nch // NX
    tokens, d = states.shape
    vw = head_weight.shape[1] // ny
    seqs, seq = positions.shape
    slots = seqs * CAP
    rg = LIVE // 4
    width = -(-(rg + 1) // 128) * 128
    dg = 256 // nch
    cfg = (ny, nx, nz, vw, slots, tokens, seq, ndp * tokens)
    dma = pltpu.SemaphoreType.DMA
    scratch = [
        pltpu.SMEM(counts.shape, jnp.int32),
        pltpu.SMEM(rate_num.shape, jnp.int32),
        pltpu.VMEM(positions.shape, jnp.int32),
        pltpu.VMEM((1, tokens), jnp.int32),
        pltpu.VMEM((2,) + head_weight.shape, BF16),
        pltpu.VMEM((tokens, 128), BF16),
        pltpu.VMEM((tokens, 128), BF16),
        pltpu.VMEM((2, ny, slots + META, 128), BF16),
        pltpu.VMEM((ndp, 128, vw), BF16),
        pltpu.VMEM((2, nch, rg // 2, 128), BF16),
        pltpu.VMEM((2, ny, 2, rg // 2, vw), BF16),
        pltpu.VMEM((2, 2, ny, rg, vw), BF16),
        pltpu.VMEM((2, 2, 2, rg // 2, 128), BF16),
        pltpu.VMEM((ndp, 128), F32),
        pltpu.VMEM((2, rg, META), F32),
        pltpu.VMEM((2, rg, ndp * 128), BF16),
        pltpu.VMEM((ny, 2, 1, width), F32),
        pltpu.VMEM((nch, 2, 1, width), F32),
        pltpu.VMEM((2, 1, 128), F32),
        pltpu.VMEM(head_weight.shape, F32),
        pltpu.VMEM((2, 256, rg), F32),
        pltpu.VMEM((2, nch, dg, rg), F32),
        pltpu.VMEM((ndp, dg, 128), F32),
        pltpu.VMEM((nch // 2, dg, 128), F32),
        dma((6,)),
        dma((2,)),
        dma,
        dma((ny,)),
        dma((2,)),
        dma((5,)),
        dma((5,)),
        dma((2,)),
        dma,
        dma((2, nz // 2, 2)),
        dma,
        dma((nz,)),
        dma((2,)),
        dma((2,)),
        dma((2, 2, ny // 2, 2)),
        dma,
        dma((2, ny)),
        dma((2,)),
        dma((2,)),
        dma,
        dma((2,)),
        dma((2,)),
        dma,
    ]
    vmem = pl.BlockSpec(memory_space=pltpu.VMEM)
    hbm = pl.BlockSpec(memory_space=pltpu.HBM)
    out_shape = (
        jax.ShapeDtypeStruct((1, 1), F32),
        jax.ShapeDtypeStruct((d // nch, tokens), BF16),
        jax.ShapeDtypeStruct(head_weight.shape, F32),
    )
    results = pl.pallas_call(
        functools.partial(kernel, cfg),
        out_shape=out_shape,
        in_specs=[hbm] * 6,
        out_specs=(vmem, vmem, hbm),
        scratch_shapes=scratch,
        compiler_params=pltpu.CompilerParams(
            collective_id=0, has_side_effects=True, vmem_limit_bytes=63 * 1024 * 1024
        ),
    )(counts, rate_num, positions, targets.reshape(1, tokens), states, head_weight)
    loss, grad_hidden, grad_weight = pl.pallas_call(
        copies,
        out_shape=out_shape,
        in_specs=[hbm] * 3,
        out_specs=(hbm,) * 3,
        scratch_shapes=[pltpu.VMEM(o.shape, o.dtype) for o in out_shape] + [dma((2, 6))],
        compiler_params=pltpu.CompilerParams(vmem_limit_bytes=63 * 1024 * 1024),
    )(*results)
    return loss[0, 0], grad_hidden.T, grad_weight


def solution(mesh):
    return jax.shard_map(
        local,
        mesh=mesh,
        in_specs=(P("dp", None), P("dp", "vocab"), P("dp"), P("dp", None), P("dp"), P("dp")),
        out_specs=(P(), P("dp", "vocab"), P("dp", "vocab")),
        check_vma=False,
    )
```

```python
import functools

import jax
import jax.numpy as jnp
from jax import lax
from jax.experimental import pallas as pl
from jax.experimental.pallas import tpu as pltpu
from jax.sharding import PartitionSpec as P

MESH = pl.DeviceIdType.MESH
F32 = jnp.float32
BF16 = jnp.bfloat16

CAP = 48
LIVE = 896
RATE_DEN = 1024
NX = 4
META = 16


def nn(a, b):
    return lax.dot_general(a, b, (((1,), (0,)), ((), ())), preferred_element_type=F32)


def nt(a, b):
    return lax.dot_general(a, b, (((1,), (1,)), ((), ())), preferred_element_type=F32)


def tn(a, b):
    return lax.dot_general(a, b, (((0,), (0,)), ((), ())), preferred_element_type=F32)


def iota(shape, dim):
    return lax.broadcasted_iota(jnp.int32, shape, dim)


def kernel(
    cfg,
    counts_hbm,
    rate_hbm,
    pos_hbm,
    tgt_hbm,
    states_hbm,
    w_hbm,
    loss_ref,
    gh_ref,
    gw_hbm,
    counts_ref,
    rate_ref,
    pos_ref,
    tgt_ref,
    w_ref,
    s_buf,
    pmt,
    blocks,
    wc,
    xg_0,
    xg_1,
    e_buf_0,
    e_buf_1,
    g_buf_0,
    g_buf_1,
    xd_0,
    xd_1,
    rank_buf,
    meta_0,
    meta_1,
    qun_0,
    qun_1,
    lse_y_0,
    lse_y_1,
    lse_xz_0,
    lse_xz_1,
    loss_buf,
    gw_ref,
    ght_0,
    ght_1,
    red_0,
    red_1,
    fin,
    u_buf,
    in_sem,
    a_sem,
    w_send,
    w_recv,
    wf_sem,
    core_send,
    core_recv,
    x_sem,
    zr_send,
    zr_recv,
    zu_send,
    zu_recv,
    xf_sem,
    e_send,
    e_recv,
    g_send,
    g_recv,
    ly_send,
    ly_recv,
    lp_send,
    lp_recv,
    r_send,
    r_recv,
    u_sem,
    out_sem,
):
    ny, nx, nz, vw, slots, tokens, seq, all_tokens, piece_rows = cfg
    ndp, nch = 2 * ny, nx * nz
    xg, e_buf, g_buf, xd = (xg_0, xg_1), (e_buf_0, e_buf_1), (g_buf_0, g_buf_1), (xd_0, xd_1)
    meta, qun, ght, red = (meta_0, meta_1), (qun_0, qun_1), (ght_0, ght_1), (red_0, red_1)
    lse_y, lse_xz = (lse_y_0, lse_y_1), (lse_xz_0, lse_xz_1)
    rps = piece_rows
    rgs = [2 * r for r in rps]
    widths = [r.shape[2] for r in lse_y]
    dg = 256 // nch

    dp = lax.axis_index("dp")
    vo = lax.axis_index("vocab")
    y, c = dp // 2, dp % 2
    x, z = vo // nz, vo % nz
    here = c * ny + y
    piece = z * nx + x
    m, h = piece // 2, piece % 2

    def rem(src, dst, send, recv, device):
        return pltpu.make_async_remote_copy(
            src_ref=src,
            dst_ref=dst,
            send_sem=send,
            recv_sem=recv,
            device_id=device,
            device_id_type=MESH,
        )

    def go(src, dst, send, recv, device):
        rem(src, dst, send, recv, device).start()

    def arrived(dst, recv):
        rem(dst, dst, recv, recv, (dp, vo)).wait_recv()

    def gone(src, send):
        rem(src, src, send, send, (dp, vo)).wait_send()

    def in_column(yy):
        return (2 * yy + c, vo)

    sibling = (2 * y + 1 - c, vo)
    peer_x = lambda xx: (dp, xx * nz + z)
    peer_z = lambda zz: (dp, x * nz + zz)

    states_slice = states_hbm.at[:, pl.ds(pl.multiple_of(m * 128, 128), 128)]
    loads = [
        pltpu.make_async_copy(src, dst, in_sem.at[i])
        for i, (src, dst) in enumerate(
            [
                (pos_hbm, pos_ref),
                (tgt_hbm, tgt_ref),
                (counts_hbm, counts_ref),
                (rate_hbm, rate_ref),
                (states_slice, s_buf),
                (w_hbm, w_ref.at[c]),
            ]
        )
    ]
    for load in loads:
        load.start()

    barrier = pltpu.get_barrier_semaphore()
    q = vo
    target_vo = 4 * y + q // (nch // 4)
    src_y, src_q0 = vo // 4, (nch // 4) * (vo % 4)
    to_self = target_vo == vo

    def signal(device):
        pl.semaphore_signal(barrier, inc=1, device_id=device, device_id_type=MESH)

    for k in range(1, ny):
        signal(in_column((y + k) % ny))
    signal(sibling)

    def signal_plane(k, carry):
        signal((dp, (vo + k) % nch))
        return carry

    lax.fori_loop(1, nch, signal_plane, 0)

    def signal_source(t, carry):
        source = (2 * src_y + t // (nch // 4), src_q0 + t % (nch // 4))

        @pl.when(jnp.logical_not((source[0] == dp) & (source[1] == vo)))
        def _():
            signal(source)

        return carry

    lax.fori_loop(0, nch // 2, signal_source, 0)

    loads[0].wait()
    lane = iota((8, 128), 1)
    pos0 = jnp.broadcast_to(pos_ref[0:1, 0:128], (8, 128))
    pos1 = jnp.broadcast_to(pos_ref[1:2, 0:128], (8, 128))
    pos1 = pltpu.roll(pos1, CAP, 1)
    tok = jnp.where(lane < CAP, pos0, jnp.where(lane < 2 * CAP, seq + pos1, -1))[0:1]
    pmt[...] = jnp.where(iota((tokens, 128), 0) == tok, 1.0, 0.0).astype(BF16)
    loads[1].wait()
    targets = tgt_ref[...]
    row16 = iota((META, tokens), 0)
    parts = jnp.where(
        row16 == 0,
        jnp.right_shift(targets, 8).astype(F32),
        jnp.where(row16 == 1, jnp.bitwise_and(targets, 255).astype(F32), 0.0),
    ).astype(BF16)
    label_rows = nn(parts, pmt[...])
    lane16 = iota((META, 128), 1)
    row16 = iota((META, 128), 0)

    def per_slot(first, second):
        return jnp.where(
            lane16 < CAP, first, jnp.where(lane16 < 2 * CAP, second, 0)
        ).astype(F32)

    loads[2].wait()
    loads[3].wait()
    r0, r1 = rate_ref[0], rate_ref[1]
    own_meta = jnp.where(
        row16 == 2, per_slot(jnp.right_shift(r0, 8), jnp.right_shift(r1, 8)), label_rows
    )
    own_meta = jnp.where(
        row16 == 3, per_slot(jnp.bitwise_and(r0, 255), jnp.bitwise_and(r1, 255)), own_meta
    )
    own_meta = jnp.where(row16 == 4, per_slot(counts_ref[0], counts_ref[1]), own_meta)
    loads[4].wait()
    chosen = tn(pmt[...], s_buf[...])
    blocks[c, y, 0:slots, :] = chosen[0:slots].astype(BF16)
    blocks[c, y, slots : slots + META, :] = own_meta.astype(BF16)

    n_to = (ny - 1) + 1 + (nch - 1)
    pl.semaphore_wait(barrier, n_to + ndp - jnp.where(to_self, 1, 0))

    for k in range(1, ny):
        go(blocks.at[c, y], blocks.at[c, y], a_sem.at[0], a_sem.at[1], in_column((y + k) % ny))
    loads[5].wait()

    def own_columns(o):
        return w_ref.at[c, :, pl.ds(pl.multiple_of(o * vw, vw), vw)]

    arrived(blocks.at[c, 0 : ny - 1], a_sem.at[1])
    go(blocks.at[c], blocks.at[c], core_send.at[0], core_recv.at[0], sibling)
    near = sorted(range(1, ny), key=lambda k: min(k, ny - k))
    for k in reversed(near):
        yy = (y + k) % ny
        go(own_columns(yy), wc.at[dp], w_send, w_recv.at[k], in_column(yy))
    wc[dp] = own_columns(y)[...]
    arrived(blocks.at[1 - c], core_recv.at[0])
    go(wc.at[dp], wc.at[dp], wf_sem.at[0], wf_sem.at[1], sibling)

    all_meta = blocks[:, :, slots : slots + META, :].astype(F32).reshape(ndp, META, 128)
    count_rows = jnp.sum(
        jnp.where(iota((ndp, META, 128), 1) == 4, all_meta, 0.0), axis=1
    )
    first, second = count_rows[:, 0:1], count_rows[:, CAP : CAP + 1]
    in_all = jnp.broadcast_to(first + second, (ndp, 128)).astype(BF16)

    def order(v):
        return 2 * (v % ny) + v // ny

    earlier = jnp.where(
        order(iota((ndp, ndp), 1)) < order(iota((ndp, ndp), 0)), 1.0, 0.0
    ).astype(BF16)
    offset = nn(earlier, in_all)
    lanes = iota((ndp, 128), 1).astype(F32)
    in_first = lanes < CAP
    place = jnp.where(in_first, lanes, lanes - CAP + first)
    bound = jnp.where(in_first, first, second)
    local_place = jnp.where(in_first, lanes, lanes - CAP)
    live = (local_place < bound) & (lanes < 2 * CAP)
    rank_buf[...] = jnp.where(live, offset + place, -1.0)

    def first_row(t):
        return c * (LIVE // 2) + (rgs[0] if t else 0)

    def one_hot(start, rows, a):
        names = iota((rows, 128), 0) + start
        return jnp.where(names.astype(F32) == rank_buf[a : a + 1, :], 1.0, 0.0).astype(BF16)

    def own_piece(t):
        rp = rps[t]
        acc = jnp.zeros((rp, 128), F32)
        for a in range(ndp):
            pick = one_hot(first_row(t) + h * rp, rp, a)
            acc += nn(pick[:, 0:slots], blocks[a // ny, a % ny, 0:slots, :])
        xg[t][piece] = acc.astype(BF16)
        return xg[t].at[piece]

    def metas(t):
        rg = rgs[t]
        total = jnp.zeros((rg, META), F32)
        for a in range(ndp):
            pick = one_hot(first_row(t), rg, a)
            qun[t][:, a * 128 : (a + 1) * 128] = pick
            total += nt(pick, blocks[a // ny, a % ny, slots : slots + META, :])
        meta[t][...] = total

    def ring(n, me, block, subs, send, recv, device):
        last = n // 2 - 1

        def moves(step):
            for sub in range(subs):
                for way in (0, 1):
                    if step < last or (sub < subs // 2) == (way == 0):
                        yield way, sub

        def start(step):
            for way, sub in moves(step):
                start_one(step, way, sub)

        def start_one(step, way, sub):
            origin = (me + n - step) % n if way == 0 else (me + step) % n
            to = (me + 1) % n if way == 0 else (me + n - 1) % n
            ref = block(origin, sub)
            go(ref, ref, send, recv.at[way, step, sub], device(to))

        def advance(step, then=None):
            following = set(moves(step + 1)) if step < last else set()
            for way, sub in moves(step):
                origin = (me + n - 1 - step) % n if way == 0 else (me + 1 + step) % n
                ref = block(origin, sub)
                arrived(ref, recv.at[way, step, sub])
                if (way, sub) in following:
                    start_one(step + 1, way, sub)
                if then is not None:
                    then((n - 1 - step) if way == 0 else 1 + step, sub)

        return last, start, advance

    half_x = nx // 2
    x_last, x_start, x_advance = ring(
        nz,
        z,
        lambda o, sub: xg[1].at[pl.ds(o * nx + sub * half_x, half_x)],
        2,
        zr_send,
        zr_recv,
        peer_z,
    )

    def pass_on(k):
        ref = xg[0].at[((z + nz - k) % nz) * nx + x]
        if k > 0:
            arrived(ref, zu_recv.at[k])
        for i in range(1, nx):
            go(ref, ref, xf_sem.at[0], xf_sem.at[1], peer_x((x + i) % nx))

    def w_arrive(k):
        ref = wc.at[2 * ((y + ny - k) % ny) + c]
        arrived(ref, w_recv.at[k])
        go(ref, ref, wf_sem.at[0], wf_sem.at[1], sibling)

    z_near = sorted(range(1, nz), key=lambda k: min(k, nz - k))
    w_near = list(near)

    def take(todo, count, do):
        for _ in range(min(count, len(todo))):
            do(todo.pop(0))

    def rows_come(step):
        if step <= x_last:
            x_advance(step)

    mine = own_piece(0)
    for k in z_near:
        go(mine, mine, zu_send, zu_recv.at[k], peer_z((z + k) % nz))
    pass_on(0)
    mine = own_piece(1)
    for k in range(1, nx):
        go(mine, mine, x_sem.at[0], x_sem.at[1], peer_x((x + k) % nx))
    arrived(xg[1].at[0 : nx - 1], x_sem.at[1])
    x_start(0)
    take(z_near, 4, pass_on)
    metas(1)
    rows_come(0)
    take(z_near, 2, pass_on)
    take(w_near, 2, w_arrive)
    rows_come(1)
    take(z_near, nz, pass_on)
    metas(0)
    take(w_near, 2, w_arrive)
    rows_come(2)
    take(w_near, ny, w_arrive)
    go(w_ref.at[c], w_ref.at[c], core_send.at[1], core_recv.at[1], sibling)
    arrived(xg[0].at[0 : (nx - 1) * nz], xf_sem.at[1])
    arrived(wc.at[0:ny], wf_sem.at[1])

    def label_of(t):
        rows = meta[t][...]
        return (rows[:, 0:1] * 256.0 + rows[:, 1:2]).astype(jnp.int32)

    def weight_of(t):
        rows = meta[t][...]
        return RATE_DEN / (rows[:, 2:3] * 256.0 + rows[:, 3:4])

    e_rings = [
        ring(
            ny,
            y,
            lambda o, sub, t=t: e_buf[t].at[o, sub],
            2,
            e_send.at[t],
            e_recv.at[t],
            in_column,
        )
        for t in range(2)
    ]
    e_last = e_rings[0][0]

    def softmax_part(t):
        rg, rp, width = rgs[t], rps[t], widths[t]
        logits = jnp.zeros((rg, vw), F32)
        for mm in range(0, ndp, 2):
            rows = [xg[t][2 * (mm + i) : 2 * (mm + i) + 2].reshape(rg, 128) for i in range(2)]
            logits += nn(
                jnp.concatenate(rows, axis=1), wc[mm : mm + 2].reshape(256, vw)
            )
        high = jnp.max(logits, axis=1, keepdims=True)
        powers = jnp.exp(logits - high)
        sums = jnp.sum(powers, axis=1, keepdims=True)
        lse = high + jnp.log(sums)
        own_part = powers * (1.0 / sums)
        for sub in range(2):
            e_buf[t][y, sub] = own_part[sub * rp : (sub + 1) * rp].astype(BF16)
        hit = iota((rg, vw), 1) == label_of(t) - (vo * (vw * ny) + y * vw)
        of_targets = jnp.sum(
            jnp.sum(jnp.where(hit, logits * weight_of(t), 0.0), axis=1, keepdims=True),
            axis=0,
            keepdims=True,
        )
        lse_row = jnp.transpose(jnp.broadcast_to(lse, (rg, 128)))[0:1]
        lse_y[t][y, :, 0:rg] = lse_row
        lse_y[t][y, :, rg:width] = jnp.broadcast_to(of_targets, (1, width - rg))
        for k in range(1, ny):
            ref = lse_y[t].at[y]
            go(ref, ref, ly_send.at[t], ly_recv.at[t], in_column((y + k) % ny))
        e_rings[t][1](0)
        go(
            xg[t].at[pl.ds(2 * (dp + 1 - 2 * c), 2)],
            xd[t].at[c],
            core_send.at[2 + t],
            core_recv.at[2 + t],
            sibling,
        )
        xd[t][c] = xg[t][pl.ds(2 * dp, 2)]

    def combine(t, rows):
        top = functools.reduce(jnp.maximum, rows)
        exps = functools.reduce(jnp.add, [jnp.exp(r - top) for r in rows])
        plain = functools.reduce(jnp.add, rows)
        in_rows = iota((1, widths[t]), 1) < rgs[t]
        return jnp.where(in_rows, top + jnp.log(exps), plain)

    def column_stats(t):
        arrived(lse_y[t].at[0 : ny - 1], ly_recv.at[t])
        lse_xz[t][vo] = combine(t, [lse_y[t][i] for i in range(ny)])

        def send(k, carry):
            ref = lse_xz[t].at[vo]
            go(ref, ref, lp_send.at[t], lp_recv.at[t], (dp, (vo + k) % nch))
            return carry

        lax.fori_loop(1, nch, send, 0)

    features, scales, labels, weights, losses = {}, {}, {}, {}, {}

    def plane_stats(t):
        rg = rgs[t]
        arrived(lse_xz[t].at[0 : nch - 1], lp_recv.at[t])
        log_total = combine(t, [lse_xz[t][i] for i in range(nch)])
        rows = [lse_y[t][(y + k) % ny] for k in range(ny)] + [log_total]
        rows += [jnp.zeros_like(log_total)] * (-len(rows) % 8)
        cols = jnp.transpose(jnp.concatenate(rows, axis=0))[0:rg]
        labels[t], weights[t] = label_of(t), weight_of(t)
        total_col = cols[:, ny : ny + 1]
        scales[t] = weights[t] * jnp.exp(cols - total_col)
        losses[t] = jnp.sum(weights[t] * total_col, axis=0, keepdims=True) - log_total[:, rg : rg + 1]
        features[t] = jnp.transpose(xd[t][c].reshape(rg, 128))
        if t == 0:
            arrived(w_ref.at[1 - c], core_recv.at[1])
        else:
            loss_buf[c] = jnp.broadcast_to(losses[0] + losses[1], loss_buf.shape[1:])
            go(loss_buf.at[c], loss_buf.at[c], core_send.at[4], core_recv.at[4], sibling)

    def own(t, offset):
        o = (y + offset) % ny
        columns = pl.ds(pl.multiple_of(o * vw, vw), vw)
        rg = rgs[t]
        part = e_buf[t][o].reshape(rg, vw).astype(F32)
        hit = iota((rg, vw), 1) == labels[t] - (vo * (vw * ny) + o * vw)
        scaled = part * scales[t][:, offset : offset + 1]
        g_logits = jnp.where(hit, scaled - weights[t], scaled).astype(BF16)
        g_buf[t][c, o] = g_logits
        go(g_buf[t].at[c, o], g_buf[t].at[c, o], g_send.at[t], g_recv.at[t, offset], sibling)
        term = nt(w_ref[:, :, columns].reshape(256, vw), g_logits)
        if offset == 0:
            ght[t][...] = term
        else:
            ght[t][...] += term
        grad = nn(features[t], g_logits)
        if t == 0:
            gw_ref[:, columns] = grad
        else:
            gw_ref[:, columns] += grad

    def others():
        for t in range(2):
            arrived(xd[t].at[1 - c], core_recv.at[2 + t])
        turned = [jnp.transpose(xd[t][1 - c].reshape(rgs[t], 128)) for t in range(2)]
        for offset in range(ny):
            o = (y + offset) % ny
            columns = pl.ds(pl.multiple_of(o * vw, vw), vw)
            grad = gw_ref[:, columns]
            for t in range(2):
                arrived(g_buf[t].at[1 - c, o], g_recv.at[t, offset])
                grad += nn(turned[t], g_buf[t][1 - c, o])
            gw_ref[:, columns] = grad

    def piece_of(t, qq):
        return ght[t].at[pl.ds(pl.multiple_of(qq * dg, dg), dg), :]

    def send_pieces(t):
        def send(k, carry):
            to = (vo + k) % nch
            go(piece_of(t, to), red[t].at[vo], r_send.at[t], r_recv.at[t], (dp, to))
            return carry

        lax.fori_loop(1, nch, send, 0)
        red[t][vo] = piece_of(t, vo)[...]

    def add_pieces(t):
        arrived(red[t].at[0 : nch - 1], r_recv.at[t])
        return nn(jnp.sum(red[t][...], axis=0).astype(BF16), qun[t][...])

    softmax_part(0)
    arrival = [sorted({ny - 1 - s, 1 + s}) for s in range(e_last + 1)]
    ready = {0: [0], 1: [0]}

    def spread(t, step):
        if step <= e_last:
            e_rings[t][2](step)
            ready[t] += arrival[step]

    def work(t, count):
        for _ in range(min(count, len(ready[t]))):
            offset = ready[t].pop(0)
            own(t, offset)
            if offset == ny // 2:
                send_pieces(t)

    rows_come(3)
    softmax_part(1)
    spread(0, 0)
    column_stats(0)
    spread(1, 0)
    column_stats(1)
    spread(0, 1)
    plane_stats(0)
    spread(1, 1)
    plane_stats(1)
    work(0, 3)
    spread(0, 2)
    work(0, 2)
    spread(1, 2)
    work(1, 3)
    spread(0, 3)
    work(0, ny)
    work(1, ny)
    spread(1, 3)
    work(1, ny)
    others()
    gw_copy = pltpu.make_async_copy(gw_ref, gw_hbm, out_sem)
    gw_copy.start()
    arrived(loss_buf.at[1 - c], core_recv.at[4])
    loss_ref[...] = (loss_buf[0, :, 0:1] + loss_buf[1, :, 0:1]) * (1.0 / all_tokens)
    in_slots = add_pieces(0)
    in_slots += add_pieces(1)
    for a in range(ndp):
        fin[a] = in_slots[:, a * 128 : (a + 1) * 128]
    slot = c * (nch // 4) + q % (nch // 4)

    def send_final(a, carry):
        @pl.when(jnp.logical_not(to_self & (a == here)))
        def _():
            to = (2 * (a % ny) + a // ny, target_vo)
            go(fin.at[a], u_buf.at[slot], u_sem.at[0], u_sem.at[1], to)

        return carry

    lax.fori_loop(0, ndp, send_final, 0)

    @pl.when(to_self)
    def _():
        u_buf[slot] = fin[here]

    gone(blocks.at[c, 0 : ny - 1], a_sem.at[0])
    gone(wc.at[0 : ny - 1], w_send)
    gone(wc.at[0:ny], wf_sem.at[0])
    gone(blocks.at[c], core_send.at[0])
    gone(w_ref.at[c], core_send.at[1])
    gone(loss_buf.at[c], core_send.at[4])
    gone(xg[1].at[0 : nx - 1], x_sem.at[0])
    gone(xg[1].at[0 : (nz - 1) * nx], zr_send)
    gone(xg[0].at[0 : nz - 1], zu_send)
    gone(xg[0].at[0 : (nx - 1) * nz], xf_sem.at[0])
    for t in range(2):
        gone(xd[t].at[c], core_send.at[2 + t])
        gone(e_buf[t].at[0 : ny - 1], e_send.at[t])
        gone(lse_y[t].at[0 : ny - 1], ly_send.at[t])
        gone(lse_xz[t].at[0 : nch - 1], lp_send.at[t])
        gone(g_buf[t].at[c], g_send.at[t])
        gone(red[t].at[0 : nch - 1], r_send.at[t])
    gw_copy.wait()

    @pl.when(to_self)
    def _():
        arrived(u_buf.at[0 : nch // 2 - 1], u_sem.at[1])
        gone(fin.at[0 : ndp - 1], u_sem.at[0])

    @pl.when(jnp.logical_not(to_self))
    def _():
        arrived(u_buf, u_sem.at[1])
        gone(fin, u_sem.at[0])

    half = nch // 4
    pieces = [u_buf[t] + u_buf[half + t] for t in range(half)]
    columns = jnp.concatenate(pieces, axis=0).astype(BF16)
    gh_ref[...] = nt(columns, pmt[...]).astype(BF16)


def copies(loss, gh, gw, loss_out, gh_out, gw_out, loss_buf, gh_buf, gw_buf, sems):
    rows = gw.shape[0] // 4
    moves = [(loss, loss_buf, loss_out), (gh, gh_buf, gh_out)]
    moves += [tuple(r.at[pl.ds(k * rows, rows)] for r in (gw, gw_buf, gw_out)) for k in range(4)]
    into = [pltpu.make_async_copy(a, b, sems.at[0, k]) for k, (a, b, _) in enumerate(moves)]
    out = [pltpu.make_async_copy(b, d, sems.at[1, k]) for k, (_, b, d) in enumerate(moves)]
    for move in into:
        move.start()
    for first, then in zip(into, out):
        first.wait()
        then.start()
    for move in out:
        move.wait()


def local(states, head_weight, targets, positions, counts, rate_num):
    ndp = lax.axis_size("dp")
    nch = lax.axis_size("vocab")
    ny, nx, nz = ndp // 2, NX, nch // NX
    tokens, d = states.shape
    vw = head_weight.shape[1] // ny
    seqs, seq = positions.shape
    slots = seqs * CAP
    rh = LIVE // 4
    first = (7 * rh // 10 + 8) // 16 * 16
    rps = (first, rh - first)
    rgs = [2 * r for r in rps]
    widths = [-(-(r + 1) // 128) * 128 for r in rgs]
    dg = 256 // nch
    cfg = (ny, nx, nz, vw, slots, tokens, seq, ndp * tokens, rps)
    dma = pltpu.SemaphoreType.DMA
    scratch = [
        pltpu.SMEM(counts.shape, jnp.int32),
        pltpu.SMEM(rate_num.shape, jnp.int32),
        pltpu.VMEM(positions.shape, jnp.int32),
        pltpu.VMEM((1, tokens), jnp.int32),
        pltpu.VMEM((2,) + head_weight.shape, BF16),
        pltpu.VMEM((tokens, 128), BF16),
        pltpu.VMEM((tokens, 128), BF16),
        pltpu.VMEM((2, ny, slots + META, 128), BF16),
        pltpu.VMEM((ndp, 128, vw), BF16),
        *[pltpu.VMEM((nch, r, 128), BF16) for r in rps],
        *[pltpu.VMEM((ny, 2, r, vw), BF16) for r in rps],
        *[pltpu.VMEM((2, ny, r, vw), BF16) for r in rgs],
        *[pltpu.VMEM((2, 2, r, 128), BF16) for r in rps],
        pltpu.VMEM((ndp, 128), F32),
        *[pltpu.VMEM((r, META), F32) for r in rgs],
        *[pltpu.VMEM((r, ndp * 128), BF16) for r in rgs],
        *[pltpu.VMEM((ny, 1, w), F32) for w in widths],
        *[pltpu.VMEM((nch, 1, w), F32) for w in widths],
        pltpu.VMEM((2, 1, 128), F32),
        pltpu.VMEM(head_weight.shape, F32),
        *[pltpu.VMEM((256, r), F32) for r in rgs],
        *[pltpu.VMEM((nch, dg, r), F32) for r in rgs],
        pltpu.VMEM((ndp, dg, 128), F32),
        pltpu.VMEM((nch // 2, dg, 128), F32),
        dma((6,)),
        dma((2,)),
        dma,
        dma((ny,)),
        dma((2,)),
        dma((5,)),
        dma((5,)),
        dma((2,)),
        dma,
        dma((2, nz // 2, 2)),
        dma,
        dma((nz,)),
        dma((2,)),
        dma((2,)),
        dma((2, 2, ny // 2, 2)),
        dma((2,)),
        dma((2, ny)),
        dma((2,)),
        dma((2,)),
        dma((2,)),
        dma((2,)),
        dma((2,)),
        dma((2,)),
        dma((2,)),
        dma,
    ]
    vmem = pl.BlockSpec(memory_space=pltpu.VMEM)
    hbm = pl.BlockSpec(memory_space=pltpu.HBM)
    out_shape = (
        jax.ShapeDtypeStruct((1, 1), F32),
        jax.ShapeDtypeStruct((d // nch, tokens), BF16),
        jax.ShapeDtypeStruct(head_weight.shape, F32),
    )
    results = pl.pallas_call(
        functools.partial(kernel, cfg),
        out_shape=out_shape,
        in_specs=[hbm] * 6,
        out_specs=(vmem, vmem, hbm),
        scratch_shapes=scratch,
        compiler_params=pltpu.CompilerParams(
            collective_id=0, has_side_effects=True, vmem_limit_bytes=63 * 1024 * 1024
        ),
    )(counts, rate_num, positions, targets.reshape(1, tokens), states, head_weight)
    loss, grad_hidden, grad_weight = pl.pallas_call(
        copies,
        out_shape=out_shape,
        in_specs=[hbm] * 3,
        out_specs=(hbm,) * 3,
        scratch_shapes=[pltpu.VMEM(o.shape, o.dtype) for o in out_shape] + [dma((2, 6))],
        compiler_params=pltpu.CompilerParams(vmem_limit_bytes=63 * 1024 * 1024),
    )(*results)
    return loss[0, 0], grad_hidden.T, grad_weight


def solution(mesh):
    return jax.shard_map(
        local,
        mesh=mesh,
        in_specs=(P("dp", None), P("dp", "vocab"), P("dp"), P("dp", None), P("dp"), P("dp")),
        out_specs=(P(), P("dp", "vocab"), P("dp", "vocab")),
        check_vma=False,
    )
```

```python
import functools

import jax
import jax.numpy as jnp
from jax import lax
from jax.experimental import pallas as pl
from jax.experimental.pallas import tpu as pltpu
from jax.sharding import PartitionSpec as P

MESH = pl.DeviceIdType.MESH
F32 = jnp.float32
BF16 = jnp.bfloat16

CAP = 48
LIVE = 896
RATE_DEN = 1024
NX = 4
META = 16


def nn(a, b):
    return lax.dot_general(a, b, (((1,), (0,)), ((), ())), preferred_element_type=F32)


def nt(a, b):
    return lax.dot_general(a, b, (((1,), (1,)), ((), ())), preferred_element_type=F32)


def tn(a, b):
    return lax.dot_general(a, b, (((0,), (0,)), ((), ())), preferred_element_type=F32)


def iota(shape, dim):
    return lax.broadcasted_iota(jnp.int32, shape, dim)


def kernel(
    cfg,
    counts_hbm,
    rate_hbm,
    pos_hbm,
    tgt_hbm,
    states_hbm,
    w_hbm,
    loss_ref,
    gh_ref,
    gw_hbm,
    counts_ref,
    rate_ref,
    pos_ref,
    tgt_ref,
    w_ref,
    s_buf,
    pmt,
    blocks,
    wc,
    xg_0,
    xg_1,
    e_buf_0,
    e_buf_1,
    g_buf_0,
    g_buf_1,
    xd_0,
    xd_1,
    rank_buf,
    meta_0,
    meta_1,
    qun_0,
    qun_1,
    lse_y_0,
    lse_y_1,
    lse_xz_0,
    lse_xz_1,
    loss_buf,
    gw_ref,
    ght_0,
    ght_1,
    red_0,
    red_1,
    fin,
    u_buf,
    in_sem,
    a_sem,
    w_send,
    w_recv,
    wf_sem,
    core_send,
    core_recv,
    x_sem,
    zr_send,
    zr_recv,
    zu_send,
    zu_recv,
    xf_sem,
    e_send,
    e_recv,
    g_send,
    g_recv,
    ly_send,
    ly_recv,
    lp_send,
    lp_recv,
    r_send,
    r_recv,
    u_sem,
    out_sem,
):
    ny, nx, nz, vw, tokens, seq, all_tokens, piece_rows = cfg
    ndp, nch = 2 * ny, nx * nz
    xg, e_buf, g_buf, xd = (xg_0, xg_1), (e_buf_0, e_buf_1), (g_buf_0, g_buf_1), (xd_0, xd_1)
    meta, qun, ght, red = (meta_0, meta_1), (qun_0, qun_1), (ght_0, ght_1), (red_0, red_1)
    lse_y, lse_xz = (lse_y_0, lse_y_1), (lse_xz_0, lse_xz_1)
    rps = piece_rows
    rgs = [2 * r for r in rps]
    widths = [r.shape[2] for r in lse_y]
    dg = 256 // nch

    dp = lax.axis_index("dp")
    vo = lax.axis_index("vocab")
    y, c = dp // 2, dp % 2
    x, z = vo // nz, vo % nz
    here = c * ny + y
    piece = z * nx + x
    m, h = piece // 2, piece % 2

    def rem(src, dst, send, recv, device):
        return pltpu.make_async_remote_copy(
            src_ref=src,
            dst_ref=dst,
            send_sem=send,
            recv_sem=recv,
            device_id=device,
            device_id_type=MESH,
        )

    def go(src, dst, send, recv, device):
        rem(src, dst, send, recv, device).start()

    def arrived(dst, recv):
        rem(dst, dst, recv, recv, (dp, vo)).wait_recv()

    def gone(src, send):
        rem(src, src, send, send, (dp, vo)).wait_send()

    def in_column(yy):
        return (2 * yy + c, vo)

    sibling = (2 * y + 1 - c, vo)
    peer_x = lambda xx: (dp, xx * nz + z)
    peer_z = lambda zz: (dp, x * nz + zz)

    states_slice = states_hbm.at[:, pl.ds(pl.multiple_of(m * 128, 128), 128)]
    loads = [
        pltpu.make_async_copy(src, dst, in_sem.at[i])
        for i, (src, dst) in enumerate(
            [
                (pos_hbm, pos_ref),
                (tgt_hbm, tgt_ref),
                (counts_hbm, counts_ref),
                (rate_hbm, rate_ref),
                (states_slice, s_buf),
                (w_hbm, w_ref.at[c]),
            ]
        )
    ]
    for load in loads:
        load.start()

    barrier = pltpu.get_barrier_semaphore()
    q = vo
    target_vo = 4 * y + q // (nch // 4)
    src_y, src_q0 = vo // 4, (nch // 4) * (vo % 4)
    to_self = target_vo == vo

    def signal(device):
        pl.semaphore_signal(barrier, inc=1, device_id=device, device_id_type=MESH)

    for k in range(1, ny):
        signal(in_column((y + k) % ny))
    signal(sibling)

    def signal_plane(k, carry):
        signal((dp, (vo + k) % nch))
        return carry

    lax.fori_loop(1, nch, signal_plane, 0)

    def signal_source(t, carry):
        source = (2 * src_y + t // (nch // 4), src_q0 + t % (nch // 4))

        @pl.when(jnp.logical_not((source[0] == dp) & (source[1] == vo)))
        def _():
            signal(source)

        return carry

    lax.fori_loop(0, nch // 2, signal_source, 0)

    loads[0].wait()
    lane = iota((8, 128), 1)
    pos0 = jnp.broadcast_to(pos_ref[0:1, 0:128], (8, 128))
    pos1 = jnp.broadcast_to(pos_ref[1:2, 0:128], (8, 128))
    pos1 = pltpu.roll(pos1, CAP, 1)
    tok = jnp.where(lane < CAP, pos0, jnp.where(lane < 2 * CAP, seq + pos1, -1))[0:1]
    pmt[...] = jnp.where(iota((tokens, 128), 0) == tok, 1.0, 0.0).astype(BF16)
    loads[1].wait()
    targets = tgt_ref[...]
    row16 = iota((META, tokens), 0)
    parts = jnp.where(
        row16 == 0,
        jnp.right_shift(targets, 8).astype(F32),
        jnp.where(row16 == 1, jnp.bitwise_and(targets, 255).astype(F32), 0.0),
    ).astype(BF16)
    label_rows = nn(parts, pmt[...])
    lane16 = iota((META, 128), 1)
    row16 = iota((META, 128), 0)

    def per_slot(first, second):
        return jnp.where(
            lane16 < CAP, first, jnp.where(lane16 < 2 * CAP, second, 0)
        ).astype(F32)

    loads[2].wait()
    loads[3].wait()
    r0, r1 = rate_ref[0], rate_ref[1]
    own_meta = jnp.where(
        row16 == 2, per_slot(jnp.right_shift(r0, 8), jnp.right_shift(r1, 8)), label_rows
    )
    own_meta = jnp.where(
        row16 == 3, per_slot(jnp.bitwise_and(r0, 255), jnp.bitwise_and(r1, 255)), own_meta
    )
    own_meta = jnp.where(row16 == 4, per_slot(counts_ref[0], counts_ref[1]), own_meta)
    loads[4].wait()
    chosen = tn(pmt[...], s_buf[...])
    def in_half(shape):
        return iota(shape, 1) // 64 == h

    def turn(v):
        return pltpu.roll(v, 64, 1)

    packed = jnp.where(in_half((CAP, 128)), chosen[0:CAP], turn(chosen[CAP : 2 * CAP]))
    blocks[c, y, 0:CAP, :] = packed.astype(BF16)
    blocks[c, y, CAP : CAP + META, :] = own_meta.astype(BF16)

    n_to = (ny - 1) + 1 + (nch - 1)
    pl.semaphore_wait(barrier, n_to + ndp - jnp.where(to_self, 1, 0))

    for k in range(1, ny):
        go(blocks.at[c, y], blocks.at[c, y], a_sem.at[0], a_sem.at[1], in_column((y + k) % ny))
    loads[5].wait()

    def own_columns(o):
        return w_ref.at[c, :, pl.ds(pl.multiple_of(o * vw, vw), vw)]

    arrived(blocks.at[c, 0 : ny - 1], a_sem.at[1])
    go(blocks.at[c], blocks.at[c], core_send.at[0], core_recv.at[0], sibling)
    near = sorted(range(1, ny), key=lambda k: min(k, ny - k))
    for k in reversed(near):
        yy = (y + k) % ny
        go(own_columns(yy), wc.at[dp], w_send, w_recv.at[k], in_column(yy))
    wc[dp] = own_columns(y)[...]
    arrived(blocks.at[1 - c], core_recv.at[0])
    go(wc.at[dp], wc.at[dp], wf_sem.at[0], wf_sem.at[1], sibling)

    all_meta = blocks[:, :, CAP : CAP + META, :].astype(F32).reshape(ndp, META, 128)
    count_rows = jnp.sum(
        jnp.where(iota((ndp, META, 128), 1) == 4, all_meta, 0.0), axis=1
    )
    first, second = count_rows[:, 0:1], count_rows[:, CAP : CAP + 1]
    in_all = jnp.broadcast_to(first + second, (ndp, 128)).astype(BF16)

    def order(v):
        return 2 * (v % ny) + v // ny

    earlier = jnp.where(
        order(iota((ndp, ndp), 1)) < order(iota((ndp, ndp), 0)), 1.0, 0.0
    ).astype(BF16)
    offset = nn(earlier, in_all)
    lanes = iota((ndp, 128), 1).astype(F32)
    in_first = lanes < CAP
    place = jnp.where(in_first, lanes, lanes - CAP + first)
    bound = jnp.where(in_first, first, second)
    local_place = jnp.where(in_first, lanes, lanes - CAP)
    live = (local_place < bound) & (lanes < 2 * CAP)
    ranks = jnp.where(live, offset + place, -1.0)
    rank_buf[0] = ranks
    rank_buf[1] = pltpu.roll(ranks, 128 - CAP, 1)

    def first_row(t):
        return c * (LIVE // 2) + (rgs[0] if t else 0)

    def one_hot(start, rows, a, second=0):
        names = iota((rows, 128), 0) + start
        return jnp.where(names.astype(F32) == rank_buf[second, a : a + 1, :], 1.0, 0.0).astype(BF16)

    def own_piece(t):
        rp, rg = rps[t], rgs[t]
        parts = [jnp.zeros((rg, 128), F32)] * 2
        for a in range(ndp):
            for i in range(2):
                pick = one_hot(first_row(t), rg, a, i)
                parts[i] += nn(pick[:, 0:CAP], blocks[a // ny, a % ny, 0:CAP, :])
        upper = parts[0][0:rp] + turn(parts[1][0:rp])
        lower = turn(parts[0][rp:rg]) + parts[1][rp:rg]
        xg[t][piece] = jnp.where(in_half((rp, 128)), upper, lower).astype(BF16)
        return xg[t].at[piece]

    def metas(t):
        rg = rgs[t]
        total = jnp.zeros((rg, META), F32)
        for a in range(ndp):
            pick = one_hot(first_row(t), rg, a)
            qun[t][:, a * 128 : (a + 1) * 128] = pick
            total += nt(pick, blocks[a // ny, a % ny, CAP : CAP + META, :])
        meta[t][...] = total

    def ring(n, me, block, subs, send, recv, device):
        last = n // 2 - 1

        def moves(step):
            for sub in range(subs):
                for way in (0, 1):
                    if step < last or (sub < subs // 2) == (way == 0):
                        yield way, sub

        def start(step):
            for way, sub in moves(step):
                start_one(step, way, sub)

        def start_one(step, way, sub):
            origin = (me + n - step) % n if way == 0 else (me + step) % n
            to = (me + 1) % n if way == 0 else (me + n - 1) % n
            ref = block(origin, sub)
            go(ref, ref, send, recv.at[way, step, sub], device(to))

        def advance(step, then=None):
            following = set(moves(step + 1)) if step < last else set()
            for way, sub in moves(step):
                origin = (me + n - 1 - step) % n if way == 0 else (me + 1 + step) % n
                ref = block(origin, sub)
                arrived(ref, recv.at[way, step, sub])
                if (way, sub) in following:
                    start_one(step + 1, way, sub)
                if then is not None:
                    then((n - 1 - step) if way == 0 else 1 + step, sub)

        return last, start, advance

    half_x = nx // 2
    x_last, x_start, x_advance = ring(
        nz,
        z,
        lambda o, sub: xg[1].at[pl.ds(o * nx + sub * half_x, half_x)],
        2,
        zr_send,
        zr_recv,
        peer_z,
    )

    def pass_on(k):
        ref = xg[0].at[((z + nz - k) % nz) * nx + x]
        if k > 0:
            arrived(ref, zu_recv.at[k])
        for i in range(1, nx):
            go(ref, ref, xf_sem.at[0], xf_sem.at[1], peer_x((x + i) % nx))

    def w_arrive(k):
        ref = wc.at[2 * ((y + ny - k) % ny) + c]
        arrived(ref, w_recv.at[k])
        go(ref, ref, wf_sem.at[0], wf_sem.at[1], sibling)

    z_near = sorted(range(1, nz), key=lambda k: min(k, nz - k))
    w_near = list(near)

    def take(todo, count, do):
        for _ in range(min(count, len(todo))):
            do(todo.pop(0))

    def rows_come(step):
        if step <= x_last:
            x_advance(step)

    mine = own_piece(0)
    for k in z_near:
        go(mine, mine, zu_send, zu_recv.at[k], peer_z((z + k) % nz))
    pass_on(0)
    mine = own_piece(1)
    for k in range(1, nx):
        go(mine, mine, x_sem.at[0], x_sem.at[1], peer_x((x + k) % nx))
    take(z_near, nz, pass_on)
    arrived(xg[1].at[0 : nx - 1], x_sem.at[1])
    x_start(0)
    metas(0)
    take(w_near, 4, w_arrive)
    rows_come(0)
    metas(1)
    take(w_near, ny, w_arrive)
    go(w_ref.at[c], w_ref.at[c], core_send.at[1], core_recv.at[1], sibling)
    arrived(xg[0].at[0 : (nx - 1) * nz], xf_sem.at[1])
    arrived(wc.at[0:ny], wf_sem.at[1])

    def label_of(t):
        rows = meta[t][...]
        return (rows[:, 0:1] * 256.0 + rows[:, 1:2]).astype(jnp.int32)

    def weight_of(t):
        rows = meta[t][...]
        return RATE_DEN / (rows[:, 2:3] * 256.0 + rows[:, 3:4])

    e_rings = [
        ring(
            ny,
            y,
            lambda o, sub, t=t: e_buf[t].at[o, sub],
            2,
            e_send.at[t],
            e_recv.at[t],
            in_column,
        )
        for t in range(2)
    ]
    e_last = e_rings[0][0]

    def rows_of(pair):
        first, second = pair[0].astype(F32), pair[1].astype(F32)
        low = iota(first.shape, 1) < 64
        upper = jnp.where(low, first, second)
        lower = turn(jnp.where(low, second, first))
        return jnp.concatenate([upper, lower], axis=0).astype(BF16)

    def softmax_part(t):
        rg, rp, width = rgs[t], rps[t], widths[t]
        logits = jnp.zeros((rg, vw), F32)
        for mm in range(0, ndp, 2):
            rows = [rows_of(xg[t][2 * (mm + i) : 2 * (mm + i) + 2]) for i in range(2)]
            logits += nn(
                jnp.concatenate(rows, axis=1), wc[mm : mm + 2].reshape(256, vw)
            )
        high = jnp.max(logits, axis=1, keepdims=True)
        powers = jnp.exp(logits - high)
        sums = jnp.sum(powers, axis=1, keepdims=True)
        lse = high + jnp.log(sums)
        own_part = powers * (1.0 / sums)
        for sub in range(2):
            e_buf[t][y, sub] = own_part[sub * rp : (sub + 1) * rp].astype(BF16)
        hit = iota((rg, vw), 1) == label_of(t) - (vo * (vw * ny) + y * vw)
        of_targets = jnp.sum(
            jnp.sum(jnp.where(hit, logits * weight_of(t), 0.0), axis=1, keepdims=True),
            axis=0,
            keepdims=True,
        )
        lse_row = jnp.transpose(jnp.broadcast_to(lse, (rg, 128)))[0:1]
        lse_y[t][y, :, 0:rg] = lse_row
        lse_y[t][y, :, rg:width] = jnp.broadcast_to(of_targets, (1, width - rg))
        for k in range(1, ny):
            ref = lse_y[t].at[y]
            go(ref, ref, ly_send.at[t], ly_recv.at[t], in_column((y + k) % ny))
        e_rings[t][1](0)
        go(
            xg[t].at[pl.ds(2 * (dp + 1 - 2 * c), 2)],
            xd[t].at[c],
            core_send.at[2 + t],
            core_recv.at[2 + t],
            sibling,
        )
        xd[t][c] = xg[t][pl.ds(2 * dp, 2)]

    def combine(t, rows):
        top = functools.reduce(jnp.maximum, rows)
        exps = functools.reduce(jnp.add, [jnp.exp(r - top) for r in rows])
        plain = functools.reduce(jnp.add, rows)
        in_rows = iota((1, widths[t]), 1) < rgs[t]
        return jnp.where(in_rows, top + jnp.log(exps), plain)

    def column_stats(t):
        arrived(lse_y[t].at[0 : ny - 1], ly_recv.at[t])
        lse_xz[t][vo] = combine(t, [lse_y[t][i] for i in range(ny)])

        def send(k, carry):
            ref = lse_xz[t].at[vo]
            go(ref, ref, lp_send.at[t], lp_recv.at[t], (dp, (vo + k) % nch))
            return carry

        lax.fori_loop(1, nch, send, 0)

    features, scales, labels, weights, losses = {}, {}, {}, {}, {}

    def plane_stats(t):
        rg = rgs[t]
        arrived(lse_xz[t].at[0 : nch - 1], lp_recv.at[t])
        log_total = combine(t, [lse_xz[t][i] for i in range(nch)])
        rows = [lse_y[t][(y + k) % ny] for k in range(ny)] + [log_total]
        rows += [jnp.zeros_like(log_total)] * (-len(rows) % 8)
        cols = jnp.transpose(jnp.concatenate(rows, axis=0))[0:rg]
        labels[t], weights[t] = label_of(t), weight_of(t)
        total_col = cols[:, ny : ny + 1]
        scales[t] = weights[t] * jnp.exp(cols - total_col)
        losses[t] = jnp.sum(weights[t] * total_col, axis=0, keepdims=True) - log_total[:, rg : rg + 1]
        features[t] = jnp.transpose(rows_of(xd[t][c]))
        if t == 0:
            arrived(w_ref.at[1 - c], core_recv.at[1])
        else:
            loss_buf[c] = jnp.broadcast_to(losses[0] + losses[1], loss_buf.shape[1:])
            go(loss_buf.at[c], loss_buf.at[c], core_send.at[4], core_recv.at[4], sibling)

    def own(t, offset):
        o = (y + offset) % ny
        columns = pl.ds(pl.multiple_of(o * vw, vw), vw)
        rg = rgs[t]
        part = e_buf[t][o].reshape(rg, vw).astype(F32)
        hit = iota((rg, vw), 1) == labels[t] - (vo * (vw * ny) + o * vw)
        scaled = part * scales[t][:, offset : offset + 1]
        g_logits = jnp.where(hit, scaled - weights[t], scaled).astype(BF16)
        g_buf[t][c, o] = g_logits
        go(g_buf[t].at[c, o], g_buf[t].at[c, o], g_send.at[t], g_recv.at[t, offset], sibling)
        term = nt(w_ref[:, :, columns].reshape(256, vw), g_logits)
        if offset == 0:
            ght[t][...] = term
        else:
            ght[t][...] += term
        grad = nn(features[t], g_logits)
        if t == 0:
            gw_ref[:, columns] = grad
        else:
            gw_ref[:, columns] += grad

    def others():
        for t in range(2):
            arrived(xd[t].at[1 - c], core_recv.at[2 + t])
        turned = [jnp.transpose(rows_of(xd[t][1 - c])) for t in range(2)]
        for offset in range(ny):
            o = (y + offset) % ny
            columns = pl.ds(pl.multiple_of(o * vw, vw), vw)
            grad = gw_ref[:, columns]
            for t in range(2):
                arrived(g_buf[t].at[1 - c, o], g_recv.at[t, offset])
                grad += nn(turned[t], g_buf[t][1 - c, o])
            gw_ref[:, columns] = grad

    def piece_of(t, qq):
        return ght[t].at[pl.ds(pl.multiple_of(qq * dg, dg), dg), :]

    def send_pieces(t):
        def send(k, carry):
            to = (vo + k) % nch
            go(piece_of(t, to), red[t].at[vo], r_send.at[t], r_recv.at[t], (dp, to))
            return carry

        lax.fori_loop(1, nch, send, 0)
        red[t][vo] = piece_of(t, vo)[...]

    def add_pieces(t):
        arrived(red[t].at[0 : nch - 1], r_recv.at[t])
        return nn(jnp.sum(red[t][...], axis=0).astype(BF16), qun[t][...])

    softmax_part(0)
    arrival = [sorted({ny - 1 - s, 1 + s}) for s in range(e_last + 1)]
    ready = {0: [0], 1: [0]}

    def spread(t, step):
        if step <= e_last:
            e_rings[t][2](step)
            ready[t] += arrival[step]

    def work(t, count):
        for _ in range(min(count, len(ready[t]))):
            offset = ready[t].pop(0)
            own(t, offset)
            if offset == ny // 2:
                send_pieces(t)

    rows_come(1)
    rows_come(2)
    spread(0, 0)
    column_stats(0)
    rows_come(3)
    softmax_part(1)
    spread(0, 1)
    plane_stats(0)
    work(0, 2)
    spread(1, 0)
    work(0, 1)
    column_stats(1)
    spread(0, 2)
    work(0, 2)
    spread(1, 1)
    spread(0, 3)
    work(0, ny)
    plane_stats(1)
    work(1, 2)
    spread(1, 2)
    work(1, ny)
    spread(1, 3)
    work(1, ny)
    others()
    gw_copy = pltpu.make_async_copy(gw_ref, gw_hbm, out_sem)
    gw_copy.start()
    arrived(loss_buf.at[1 - c], core_recv.at[4])
    loss_ref[...] = (loss_buf[0, :, 0:1] + loss_buf[1, :, 0:1]) * (1.0 / all_tokens)
    in_slots = add_pieces(0)
    in_slots += add_pieces(1)
    for a in range(ndp):
        fin[a] = in_slots[:, a * 128 : (a + 1) * 128]
    slot = c * (nch // 4) + q % (nch // 4)

    def send_final(a, carry):
        @pl.when(jnp.logical_not(to_self & (a == here)))
        def _():
            to = (2 * (a % ny) + a // ny, target_vo)
            go(fin.at[a], u_buf.at[slot], u_sem.at[0], u_sem.at[1], to)

        return carry

    lax.fori_loop(0, ndp, send_final, 0)

    @pl.when(to_self)
    def _():
        u_buf[slot] = fin[here]

    gone(blocks.at[c, 0 : ny - 1], a_sem.at[0])
    gone(wc.at[0 : ny - 1], w_send)
    gone(wc.at[0:ny], wf_sem.at[0])
    gone(blocks.at[c], core_send.at[0])
    gone(w_ref.at[c], core_send.at[1])
    gone(loss_buf.at[c], core_send.at[4])
    gone(xg[1].at[0 : nx - 1], x_sem.at[0])
    gone(xg[1].at[0 : (nz - 1) * nx], zr_send)
    gone(xg[0].at[0 : nz - 1], zu_send)
    gone(xg[0].at[0 : (nx - 1) * nz], xf_sem.at[0])
    for t in range(2):
        gone(xd[t].at[c], core_send.at[2 + t])
        gone(e_buf[t].at[0 : ny - 1], e_send.at[t])
        gone(lse_y[t].at[0 : ny - 1], ly_send.at[t])
        gone(lse_xz[t].at[0 : nch - 1], lp_send.at[t])
        gone(g_buf[t].at[c], g_send.at[t])
        gone(red[t].at[0 : nch - 1], r_send.at[t])
    gw_copy.wait()

    @pl.when(to_self)
    def _():
        arrived(u_buf.at[0 : nch // 2 - 1], u_sem.at[1])
        gone(fin.at[0 : ndp - 1], u_sem.at[0])

    @pl.when(jnp.logical_not(to_self))
    def _():
        arrived(u_buf, u_sem.at[1])
        gone(fin, u_sem.at[0])

    half = nch // 4
    pieces = [u_buf[t] + u_buf[half + t] for t in range(half)]
    columns = jnp.concatenate(pieces, axis=0).astype(BF16)
    gh_ref[...] = nt(columns, pmt[...]).astype(BF16)


def copies(loss, gh, gw, loss_out, gh_out, gw_out, loss_buf, gh_buf, gw_buf, sems):
    rows = gw.shape[0] // 4
    moves = [(loss, loss_buf, loss_out), (gh, gh_buf, gh_out)]
    moves += [tuple(r.at[pl.ds(k * rows, rows)] for r in (gw, gw_buf, gw_out)) for k in range(4)]
    into = [pltpu.make_async_copy(a, b, sems.at[0, k]) for k, (a, b, _) in enumerate(moves)]
    out = [pltpu.make_async_copy(b, d, sems.at[1, k]) for k, (_, b, d) in enumerate(moves)]
    for move in into:
        move.start()
    for first, then in zip(into, out):
        first.wait()
        then.start()
    for move in out:
        move.wait()


def local(states, head_weight, targets, positions, counts, rate_num):
    ndp = lax.axis_size("dp")
    nch = lax.axis_size("vocab")
    ny, nx, nz = ndp // 2, NX, nch // NX
    tokens, d = states.shape
    vw = head_weight.shape[1] // ny
    seq = positions.shape[1]
    rh = LIVE // 4
    first = (rh // 2 + 8) // 16 * 16
    rps = (first, rh - first)
    rgs = [2 * r for r in rps]
    widths = [-(-(r + 1) // 128) * 128 for r in rgs]
    dg = 256 // nch
    cfg = (ny, nx, nz, vw, tokens, seq, ndp * tokens, rps)
    dma = pltpu.SemaphoreType.DMA
    scratch = [
        pltpu.SMEM(counts.shape, jnp.int32),
        pltpu.SMEM(rate_num.shape, jnp.int32),
        pltpu.VMEM(positions.shape, jnp.int32),
        pltpu.VMEM((1, tokens), jnp.int32),
        pltpu.VMEM((2,) + head_weight.shape, BF16),
        pltpu.VMEM((tokens, 128), BF16),
        pltpu.VMEM((tokens, 128), BF16),
        pltpu.VMEM((2, ny, CAP + META, 128), BF16),
        pltpu.VMEM((ndp, 128, vw), BF16),
        *[pltpu.VMEM((nch, r, 128), BF16) for r in rps],
        *[pltpu.VMEM((ny, 2, r, vw), BF16) for r in rps],
        *[pltpu.VMEM((2, ny, r, vw), BF16) for r in rgs],
        *[pltpu.VMEM((2, 2, r, 128), BF16) for r in rps],
        pltpu.VMEM((2, ndp, 128), F32),
        *[pltpu.VMEM((r, META), F32) for r in rgs],
        *[pltpu.VMEM((r, ndp * 128), BF16) for r in rgs],
        *[pltpu.VMEM((ny, 1, w), F32) for w in widths],
        *[pltpu.VMEM((nch, 1, w), F32) for w in widths],
        pltpu.VMEM((2, 1, 128), F32),
        pltpu.VMEM(head_weight.shape, F32),
        *[pltpu.VMEM((256, r), F32) for r in rgs],
        *[pltpu.VMEM((nch, dg, r), F32) for r in rgs],
        pltpu.VMEM((ndp, dg, 128), F32),
        pltpu.VMEM((nch // 2, dg, 128), F32),
        dma((6,)),
        dma((2,)),
        dma,
        dma((ny,)),
        dma((2,)),
        dma((5,)),
        dma((5,)),
        dma((2,)),
        dma,
        dma((2, nz // 2, 2)),
        dma,
        dma((nz,)),
        dma((2,)),
        dma((2,)),
        dma((2, 2, ny // 2, 2)),
        dma((2,)),
        dma((2, ny)),
        dma((2,)),
        dma((2,)),
        dma((2,)),
        dma((2,)),
        dma((2,)),
        dma((2,)),
        dma((2,)),
        dma,
    ]
    vmem = pl.BlockSpec(memory_space=pltpu.VMEM)
    hbm = pl.BlockSpec(memory_space=pltpu.HBM)
    out_shape = (
        jax.ShapeDtypeStruct((1, 1), F32),
        jax.ShapeDtypeStruct((d // nch, tokens), BF16),
        jax.ShapeDtypeStruct(head_weight.shape, F32),
    )
    results = pl.pallas_call(
        functools.partial(kernel, cfg),
        out_shape=out_shape,
        in_specs=[hbm] * 6,
        out_specs=(vmem, vmem, hbm),
        scratch_shapes=scratch,
        compiler_params=pltpu.CompilerParams(
            collective_id=0, has_side_effects=True, vmem_limit_bytes=63 * 1024 * 1024
        ),
    )(counts, rate_num, positions, targets.reshape(1, tokens), states, head_weight)
    loss, grad_hidden, grad_weight = pl.pallas_call(
        copies,
        out_shape=out_shape,
        in_specs=[hbm] * 3,
        out_specs=(hbm,) * 3,
        scratch_shapes=[pltpu.VMEM(o.shape, o.dtype) for o in out_shape] + [dma((2, 6))],
        compiler_params=pltpu.CompilerParams(vmem_limit_bytes=63 * 1024 * 1024),
    )(*results)
    return loss[0, 0], grad_hidden.T, grad_weight


def solution(mesh):
    return jax.shard_map(
        local,
        mesh=mesh,
        in_specs=(P("dp", None), P("dp", "vocab"), P("dp"), P("dp", None), P("dp"), P("dp")),
        out_specs=(P(), P("dp", "vocab"), P("dp", "vocab")),
        check_vma=False,
    )
```

```python
import functools

import jax
import jax.numpy as jnp
from jax import lax
from jax.experimental import pallas as pl
from jax.experimental.pallas import tpu as pltpu
from jax.sharding import PartitionSpec as P

MESH = pl.DeviceIdType.MESH
F32 = jnp.float32
BF16 = jnp.bfloat16

CAP = 48
LIVE = 896
RATE_DEN = 1024
NX = 4
META = 16


def nn(a, b):
    return lax.dot_general(a, b, (((1,), (0,)), ((), ())), preferred_element_type=F32)


def nt(a, b):
    return lax.dot_general(a, b, (((1,), (1,)), ((), ())), preferred_element_type=F32)


def tn(a, b):
    return lax.dot_general(a, b, (((0,), (0,)), ((), ())), preferred_element_type=F32)


def iota(shape, dim):
    return lax.broadcasted_iota(jnp.int32, shape, dim)


def kernel(
    cfg,
    counts_hbm,
    rate_hbm,
    pos_hbm,
    tgt_hbm,
    states_hbm,
    w_hbm,
    loss_ref,
    gh_ref,
    gw_hbm,
    counts_ref,
    rate_ref,
    pos_ref,
    tgt_ref,
    w_ref,
    s_buf,
    pmt,
    blocks,
    wc,
    xg_0,
    xg_1,
    e_buf_0,
    e_buf_1,
    g_buf_0,
    g_buf_1,
    xd_0,
    xd_1,
    rank_buf,
    meta_0,
    meta_1,
    qun_0,
    qun_1,
    lse_y_0,
    lse_y_1,
    lse_xz_0,
    lse_xz_1,
    loss_buf,
    gw_ref,
    ght_0,
    ght_1,
    red_0,
    red_1,
    fin,
    u_buf,
    in_sem,
    a_sem,
    w_send,
    w_recv,
    wf_sem,
    core_send,
    core_recv,
    x_sem,
    zr_send,
    zr_recv,
    zu_send,
    zu_recv,
    xf_sem,
    e_send,
    e_recv,
    g_send,
    g_recv,
    ly_send,
    ly_recv,
    lp_send,
    lp_recv,
    r_send,
    r_recv,
    u_sem,
    out_sem,
):
    ny, nx, nz, vw, tokens, seq, all_tokens, piece_rows = cfg
    ndp, nch = 2 * ny, nx * nz
    xg, e_buf, g_buf, xd = (xg_0, xg_1), (e_buf_0, e_buf_1), (g_buf_0, g_buf_1), (xd_0, xd_1)
    meta, qun, ght, red = (meta_0, meta_1), (qun_0, qun_1), (ght_0, ght_1), (red_0, red_1)
    lse_y, lse_xz = (lse_y_0, lse_y_1), (lse_xz_0, lse_xz_1)
    rps = piece_rows
    rgs = [2 * r for r in rps]
    widths = [r.shape[2] for r in lse_y]
    dg = 256 // nch

    dp = lax.axis_index("dp")
    vo = lax.axis_index("vocab")
    y, c = dp // 2, dp % 2
    x, z = vo // nz, vo % nz
    here = c * ny + y
    piece = z * nx + x
    m, h = piece // 2, piece % 2

    def rem(src, dst, send, recv, device):
        return pltpu.make_async_remote_copy(
            src_ref=src,
            dst_ref=dst,
            send_sem=send,
            recv_sem=recv,
            device_id=device,
            device_id_type=MESH,
        )

    def go(src, dst, send, recv, device):
        rem(src, dst, send, recv, device).start()

    def arrived(dst, recv):
        rem(dst, dst, recv, recv, (dp, vo)).wait_recv()

    def gone(src, send):
        rem(src, src, send, send, (dp, vo)).wait_send()

    def in_column(yy):
        return (2 * yy + c, vo)

    sibling = (2 * y + 1 - c, vo)
    peer_x = lambda xx: (dp, xx * nz + z)
    peer_z = lambda zz: (dp, x * nz + zz)

    states_slice = states_hbm.at[:, pl.ds(pl.multiple_of(m * 128, 128), 128)]
    loads = [
        pltpu.make_async_copy(src, dst, in_sem.at[i])
        for i, (src, dst) in enumerate(
            [
                (pos_hbm, pos_ref),
                (tgt_hbm, tgt_ref),
                (counts_hbm, counts_ref),
                (rate_hbm, rate_ref),
                (states_slice, s_buf),
                (w_hbm, w_ref.at[c]),
            ]
        )
    ]
    for load in loads:
        load.start()

    barrier = pltpu.get_barrier_semaphore()
    q = vo
    target_vo = 4 * y + q // (nch // 4)
    src_y, src_q0 = vo // 4, (nch // 4) * (vo % 4)
    to_self = target_vo == vo

    def signal(device):
        pl.semaphore_signal(barrier, inc=1, device_id=device, device_id_type=MESH)

    for k in range(1, ny):
        signal(in_column((y + k) % ny))
    signal(sibling)

    def signal_plane(k, carry):
        signal((dp, (vo + k) % nch))
        return carry

    lax.fori_loop(1, nch, signal_plane, 0)

    def signal_source(t, carry):
        source = (2 * src_y + t // (nch // 4), src_q0 + t % (nch // 4))

        @pl.when(jnp.logical_not((source[0] == dp) & (source[1] == vo)))
        def _():
            signal(source)

        return carry

    lax.fori_loop(0, nch // 2, signal_source, 0)

    loads[0].wait()
    lane = iota((8, 128), 1)
    pos0 = jnp.broadcast_to(pos_ref[0:1, 0:128], (8, 128))
    pos1 = jnp.broadcast_to(pos_ref[1:2, 0:128], (8, 128))
    pos1 = pltpu.roll(pos1, CAP, 1)
    tok = jnp.where(lane < CAP, pos0, jnp.where(lane < 2 * CAP, seq + pos1, -1))[0:1]
    pmt[...] = jnp.where(iota((tokens, 128), 0) == tok, 1.0, 0.0).astype(BF16)
    loads[1].wait()
    targets = tgt_ref[...]
    row16 = iota((META, tokens), 0)
    parts = jnp.where(
        row16 == 0,
        jnp.right_shift(targets, 8).astype(F32),
        jnp.where(row16 == 1, jnp.bitwise_and(targets, 255).astype(F32), 0.0),
    ).astype(BF16)
    label_rows = nn(parts, pmt[...])
    lane16 = iota((META, 128), 1)
    row16 = iota((META, 128), 0)

    def per_slot(first, second):
        return jnp.where(
            lane16 < CAP, first, jnp.where(lane16 < 2 * CAP, second, 0)
        ).astype(F32)

    loads[2].wait()
    loads[3].wait()
    r0, r1 = rate_ref[0], rate_ref[1]
    own_meta = jnp.where(
        row16 == 2, per_slot(jnp.right_shift(r0, 8), jnp.right_shift(r1, 8)), label_rows
    )
    own_meta = jnp.where(
        row16 == 3, per_slot(jnp.bitwise_and(r0, 255), jnp.bitwise_and(r1, 255)), own_meta
    )
    own_meta = jnp.where(row16 == 4, per_slot(counts_ref[0], counts_ref[1]), own_meta)
    loads[4].wait()
    chosen = tn(pmt[...], s_buf[...])
    def in_half(shape):
        return iota(shape, 1) // 64 == h

    def turn(v):
        return pltpu.roll(v, 64, 1)

    packed = jnp.where(in_half((CAP, 128)), chosen[0:CAP], turn(chosen[CAP : 2 * CAP]))
    blocks[c, y, 0:CAP, :] = packed.astype(BF16)
    blocks[c, y, CAP : CAP + META, :] = own_meta.astype(BF16)

    n_to = (ny - 1) + 1 + (nch - 1)
    pl.semaphore_wait(barrier, n_to + ndp - jnp.where(to_self, 1, 0))

    for k in range(1, ny):
        go(blocks.at[c, y], blocks.at[c, y], a_sem.at[0], a_sem.at[1], in_column((y + k) % ny))
    loads[5].wait()

    def own_columns(o):
        return w_ref.at[c, :, pl.ds(pl.multiple_of(o * vw, vw), vw)]

    arrived(blocks.at[c, 0 : ny - 1], a_sem.at[1])
    go(blocks.at[c], blocks.at[c], core_send.at[0], core_recv.at[0], sibling)
    near = sorted(range(1, ny), key=lambda k: min(k, ny - k))
    for k in reversed(near):
        yy = (y + k) % ny
        go(own_columns(yy), wc.at[dp], w_send, w_recv.at[k], in_column(yy))
    wc[dp] = own_columns(y)[...]
    arrived(blocks.at[1 - c], core_recv.at[0])
    go(wc.at[dp], wc.at[dp], wf_sem.at[0], wf_sem.at[1], sibling)

    all_meta = blocks[:, :, CAP : CAP + META, :].astype(F32).reshape(ndp, META, 128)
    count_rows = jnp.sum(
        jnp.where(iota((ndp, META, 128), 1) == 4, all_meta, 0.0), axis=1
    )
    first, second = count_rows[:, 0:1], count_rows[:, CAP : CAP + 1]
    in_all = jnp.broadcast_to(first + second, (ndp, 128)).astype(BF16)

    def order(v):
        return 2 * (v % ny) + v // ny

    earlier = jnp.where(
        order(iota((ndp, ndp), 1)) < order(iota((ndp, ndp), 0)), 1.0, 0.0
    ).astype(BF16)
    offset = nn(earlier, in_all)
    lanes = iota((ndp, 128), 1).astype(F32)
    in_first = lanes < CAP
    place = jnp.where(in_first, lanes, lanes - CAP + first)
    bound = jnp.where(in_first, first, second)
    local_place = jnp.where(in_first, lanes, lanes - CAP)
    live = (local_place < bound) & (lanes < 2 * CAP)
    ranks = jnp.where(live, offset + place, -1.0)
    rank_buf[0] = ranks
    rank_buf[1] = pltpu.roll(ranks, 128 - CAP, 1)

    def first_row(t):
        return c * (LIVE // 2) + (rgs[0] if t else 0)

    def one_hot(start, rows, a, second=0):
        names = iota((rows, 128), 0) + start
        return jnp.where(names.astype(F32) == rank_buf[second, a : a + 1, :], 1.0, 0.0).astype(BF16)

    def own_piece(t):
        rp, rg = rps[t], rgs[t]
        parts = [jnp.zeros((rg, 128), F32)] * 2
        for a in range(ndp):
            for i in range(2):
                pick = one_hot(first_row(t), rg, a, i)
                parts[i] += nn(pick[:, 0:CAP], blocks[a // ny, a % ny, 0:CAP, :])
        upper = parts[0][0:rp] + turn(parts[1][0:rp])
        lower = turn(parts[0][rp:rg]) + parts[1][rp:rg]
        xg[t][piece] = jnp.where(in_half((rp, 128)), upper, lower).astype(BF16)
        return xg[t].at[piece]

    def metas(t):
        rg = rgs[t]
        total = jnp.zeros((rg, META), F32)
        for a in range(ndp):
            pick = one_hot(first_row(t), rg, a)
            qun[t][:, a * 128 : (a + 1) * 128] = pick
            total += nt(pick, blocks[a // ny, a % ny, CAP : CAP + META, :])
        meta[t][...] = total

    def ring(n, me, block, subs, send, recv, device):
        last = n // 2 - 1

        def moves(step):
            for sub in range(subs):
                for way in (0, 1):
                    if step < last or (sub < subs // 2) == (way == 0):
                        yield way, sub

        def start(step):
            for way, sub in moves(step):
                start_one(step, way, sub)

        def start_one(step, way, sub):
            origin = (me + n - step) % n if way == 0 else (me + step) % n
            to = (me + 1) % n if way == 0 else (me + n - 1) % n
            ref = block(origin, sub)
            go(ref, ref, send, recv.at[way, step, sub], device(to))

        def advance(step, then=None):
            following = set(moves(step + 1)) if step < last else set()
            for way, sub in moves(step):
                origin = (me + n - 1 - step) % n if way == 0 else (me + 1 + step) % n
                ref = block(origin, sub)
                arrived(ref, recv.at[way, step, sub])
                if (way, sub) in following:
                    start_one(step + 1, way, sub)
                if then is not None:
                    then((n - 1 - step) if way == 0 else 1 + step, sub)

        return last, start, advance

    half_x = nx // 2
    x_last, x_start, x_advance = ring(
        nz,
        z,
        lambda o, sub: xg[1].at[pl.ds(o * nx + sub * half_x, half_x)],
        2,
        zr_send,
        zr_recv,
        peer_z,
    )

    def pass_on(k):
        ref = xg[0].at[((z + nz - k) % nz) * nx + x]
        if k > 0:
            arrived(ref, zu_recv.at[k])
        for i in range(1, nx):
            go(ref, ref, xf_sem.at[0], xf_sem.at[1], peer_x((x + i) % nx))

    def w_arrive(k):
        ref = wc.at[2 * ((y + ny - k) % ny) + c]
        arrived(ref, w_recv.at[k])
        go(ref, ref, wf_sem.at[0], wf_sem.at[1], sibling)

    z_near = sorted(range(1, nz), key=lambda k: min(k, nz - k))
    w_near = list(near)

    def take(todo, count, do):
        for _ in range(min(count, len(todo))):
            do(todo.pop(0))

    def rows_come(step):
        if step <= x_last:
            x_advance(step)

    mine = own_piece(0)
    for k in z_near:
        go(mine, mine, zu_send, zu_recv.at[k], peer_z((z + k) % nz))
    pass_on(0)
    mine = own_piece(1)
    for k in range(1, nx):
        go(mine, mine, x_sem.at[0], x_sem.at[1], peer_x((x + k) % nx))
    take(z_near, 4, pass_on)
    arrived(xg[1].at[0 : nx - 1], x_sem.at[1])
    x_start(0)
    take(z_near, nz, pass_on)
    metas(0)
    take(w_near, 4, w_arrive)
    rows_come(0)
    metas(1)
    take(w_near, ny, w_arrive)
    go(w_ref.at[c], w_ref.at[c], core_send.at[1], core_recv.at[1], sibling)
    arrived(xg[0].at[0 : (nx - 1) * nz], xf_sem.at[1])
    arrived(wc.at[0:ny], wf_sem.at[1])

    def label_of(t):
        rows = meta[t][...]
        return (rows[:, 0:1] * 256.0 + rows[:, 1:2]).astype(jnp.int32)

    def weight_of(t):
        rows = meta[t][...]
        return RATE_DEN / (rows[:, 2:3] * 256.0 + rows[:, 3:4])

    e_rings = [
        ring(
            ny,
            y,
            lambda o, sub, t=t: e_buf[t].at[o, sub],
            2,
            e_send.at[t],
            e_recv.at[t],
            in_column,
        )
        for t in range(2)
    ]
    e_last = e_rings[0][0]

    def rows_of(pair):
        first, second = pair[0].astype(F32), pair[1].astype(F32)
        low = iota(first.shape, 1) < 64
        upper = jnp.where(low, first, second)
        lower = turn(jnp.where(low, second, first))
        return jnp.concatenate([upper, lower], axis=0).astype(BF16)

    def softmax_part(t):
        rg, rp, width = rgs[t], rps[t], widths[t]
        logits = jnp.zeros((rg, vw), F32)
        for mm in range(0, ndp, 2):
            rows = [rows_of(xg[t][2 * (mm + i) : 2 * (mm + i) + 2]) for i in range(2)]
            logits += nn(
                jnp.concatenate(rows, axis=1), wc[mm : mm + 2].reshape(256, vw)
            )
        high = jnp.max(logits, axis=1, keepdims=True)
        powers = jnp.exp(logits - high)
        sums = jnp.sum(powers, axis=1, keepdims=True)
        lse = high + jnp.log(sums)
        own_part = powers * (1.0 / sums)
        for sub in range(2):
            e_buf[t][y, sub] = own_part[sub * rp : (sub + 1) * rp].astype(BF16)
        hit = iota((rg, vw), 1) == label_of(t) - (vo * (vw * ny) + y * vw)
        of_targets = jnp.sum(
            jnp.sum(jnp.where(hit, logits * weight_of(t), 0.0), axis=1, keepdims=True),
            axis=0,
            keepdims=True,
        )
        lse_row = jnp.transpose(jnp.broadcast_to(lse, (rg, 128)))[0:1]
        lse_y[t][y, :, 0:rg] = lse_row
        lse_y[t][y, :, rg:width] = jnp.broadcast_to(of_targets, (1, width - rg))
        for k in range(1, ny):
            ref = lse_y[t].at[y]
            go(ref, ref, ly_send.at[t], ly_recv.at[t], in_column((y + k) % ny))
        e_rings[t][1](0)
        go(
            xg[t].at[pl.ds(2 * (dp + 1 - 2 * c), 2)],
            xd[t].at[c],
            core_send.at[2 + t],
            core_recv.at[2 + t],
            sibling,
        )
        xd[t][c] = xg[t][pl.ds(2 * dp, 2)]

    def combine(t, rows):
        top = functools.reduce(jnp.maximum, rows)
        exps = functools.reduce(jnp.add, [jnp.exp(r - top) for r in rows])
        plain = functools.reduce(jnp.add, rows)
        in_rows = iota((1, widths[t]), 1) < rgs[t]
        return jnp.where(in_rows, top + jnp.log(exps), plain)

    def column_stats(t):
        arrived(lse_y[t].at[0 : ny - 1], ly_recv.at[t])
        lse_xz[t][vo] = combine(t, [lse_y[t][i] for i in range(ny)])

        def send(k, carry):
            ref = lse_xz[t].at[vo]
            go(ref, ref, lp_send.at[t], lp_recv.at[t], (dp, (vo + k) % nch))
            return carry

        lax.fori_loop(1, nch, send, 0)

    features, scales, labels, weights, losses = {}, {}, {}, {}, {}

    def plane_stats(t):
        rg = rgs[t]
        arrived(lse_xz[t].at[0 : nch - 1], lp_recv.at[t])
        log_total = combine(t, [lse_xz[t][i] for i in range(nch)])
        rows = [lse_y[t][(y + k) % ny] for k in range(ny)] + [log_total]
        rows += [jnp.zeros_like(log_total)] * (-len(rows) % 8)
        cols = jnp.transpose(jnp.concatenate(rows, axis=0))[0:rg]
        labels[t], weights[t] = label_of(t), weight_of(t)
        total_col = cols[:, ny : ny + 1]
        scales[t] = weights[t] * jnp.exp(cols - total_col)
        losses[t] = jnp.sum(weights[t] * total_col, axis=0, keepdims=True) - log_total[:, rg : rg + 1]
        features[t] = jnp.transpose(rows_of(xd[t][c]))
        if t == 0:
            arrived(w_ref.at[1 - c], core_recv.at[1])
        else:
            loss_buf[c] = jnp.broadcast_to(losses[0] + losses[1], loss_buf.shape[1:])
            go(loss_buf.at[c], loss_buf.at[c], core_send.at[4], core_recv.at[4], sibling)

    def own(t, offset):
        o = (y + offset) % ny
        columns = pl.ds(pl.multiple_of(o * vw, vw), vw)
        rg = rgs[t]
        part = e_buf[t][o].reshape(rg, vw).astype(F32)
        hit = iota((rg, vw), 1) == labels[t] - (vo * (vw * ny) + o * vw)
        scaled = part * scales[t][:, offset : offset + 1]
        g_logits = jnp.where(hit, scaled - weights[t], scaled).astype(BF16)
        g_buf[t][c, o] = g_logits
        go(g_buf[t].at[c, o], g_buf[t].at[c, o], g_send.at[t], g_recv.at[t, offset], sibling)
        term = nt(w_ref[:, :, columns].reshape(256, vw), g_logits)
        if offset == 0:
            ght[t][...] = term
        else:
            ght[t][...] += term
        grad = nn(features[t], g_logits)
        if t == 0:
            gw_ref[:, columns] = grad
        else:
            gw_ref[:, columns] += grad

    def others():
        for t in range(2):
            arrived(xd[t].at[1 - c], core_recv.at[2 + t])
        turned = [jnp.transpose(rows_of(xd[t][1 - c])) for t in range(2)]
        for offset in range(ny):
            o = (y + offset) % ny
            columns = pl.ds(pl.multiple_of(o * vw, vw), vw)
            grad = gw_ref[:, columns]
            for t in range(2):
                arrived(g_buf[t].at[1 - c, o], g_recv.at[t, offset])
                grad += nn(turned[t], g_buf[t][1 - c, o])
            gw_ref[:, columns] = grad

    def piece_of(t, qq):
        return ght[t].at[pl.ds(pl.multiple_of(qq * dg, dg), dg), :]

    def send_pieces(t):
        def send(k, carry):
            to = (vo + k) % nch
            go(piece_of(t, to), red[t].at[vo], r_send.at[t], r_recv.at[t], (dp, to))
            return carry

        lax.fori_loop(1, nch, send, 0)
        red[t][vo] = piece_of(t, vo)[...]

    def add_pieces(t):
        arrived(red[t].at[0 : nch - 1], r_recv.at[t])
        return nn(jnp.sum(red[t][...], axis=0).astype(BF16), qun[t][...])

    softmax_part(0)
    arrival = [sorted({ny - 1 - s, 1 + s}) for s in range(e_last + 1)]
    ready = {0: [0], 1: [0]}

    def spread(t, step):
        if step <= e_last:
            e_rings[t][2](step)
            ready[t] += arrival[step]

    def work(t, count):
        for _ in range(min(count, len(ready[t]))):
            offset = ready[t].pop(0)
            own(t, offset)
            if offset == ny // 2:
                send_pieces(t)

    rows_come(1)
    rows_come(2)
    spread(0, 0)
    column_stats(0)
    rows_come(3)
    softmax_part(1)
    spread(0, 1)
    plane_stats(0)
    work(0, 2)
    spread(1, 0)
    work(0, 1)
    column_stats(1)
    spread(0, 2)
    work(0, 2)
    spread(1, 1)
    spread(0, 3)
    work(0, ny)
    plane_stats(1)
    work(1, 2)
    spread(1, 2)
    work(1, ny)
    spread(1, 3)
    work(1, ny)
    others()
    gw_copy = pltpu.make_async_copy(gw_ref, gw_hbm, out_sem)
    gw_copy.start()
    arrived(loss_buf.at[1 - c], core_recv.at[4])
    loss_ref[...] = (loss_buf[0, :, 0:1] + loss_buf[1, :, 0:1]) * (1.0 / all_tokens)
    in_slots = add_pieces(0)
    in_slots += add_pieces(1)
    for a in range(ndp):
        fin[a] = in_slots[:, a * 128 : (a + 1) * 128]
    slot = c * (nch // 4) + q % (nch // 4)

    def send_final(a, carry):
        @pl.when(jnp.logical_not(to_self & (a == here)))
        def _():
            to = (2 * (a % ny) + a // ny, target_vo)
            go(fin.at[a], u_buf.at[slot], u_sem.at[0], u_sem.at[1], to)

        return carry

    lax.fori_loop(0, ndp, send_final, 0)

    @pl.when(to_self)
    def _():
        u_buf[slot] = fin[here]

    gone(blocks.at[c, 0 : ny - 1], a_sem.at[0])
    gone(wc.at[0 : ny - 1], w_send)
    gone(wc.at[0:ny], wf_sem.at[0])
    gone(blocks.at[c], core_send.at[0])
    gone(w_ref.at[c], core_send.at[1])
    gone(loss_buf.at[c], core_send.at[4])
    gone(xg[1].at[0 : nx - 1], x_sem.at[0])
    gone(xg[1].at[0 : (nz - 1) * nx], zr_send)
    gone(xg[0].at[0 : nz - 1], zu_send)
    gone(xg[0].at[0 : (nx - 1) * nz], xf_sem.at[0])
    for t in range(2):
        gone(xd[t].at[c], core_send.at[2 + t])
        gone(e_buf[t].at[0 : ny - 1], e_send.at[t])
        gone(lse_y[t].at[0 : ny - 1], ly_send.at[t])
        gone(lse_xz[t].at[0 : nch - 1], lp_send.at[t])
        gone(g_buf[t].at[c], g_send.at[t])
        gone(red[t].at[0 : nch - 1], r_send.at[t])
    gw_copy.wait()

    @pl.when(to_self)
    def _():
        arrived(u_buf.at[0 : nch // 2 - 1], u_sem.at[1])
        gone(fin.at[0 : ndp - 1], u_sem.at[0])

    @pl.when(jnp.logical_not(to_self))
    def _():
        arrived(u_buf, u_sem.at[1])
        gone(fin, u_sem.at[0])

    half = nch // 4
    pieces = [u_buf[t] + u_buf[half + t] for t in range(half)]
    columns = jnp.concatenate(pieces, axis=0).astype(BF16)
    gh_ref[...] = nt(columns, pmt[...]).astype(BF16)


def copies(loss, gh, gw, loss_out, gh_out, gw_out, loss_buf, gh_buf, gw_buf, sems):
    rows = gw.shape[0] // 4
    moves = [(loss, loss_buf, loss_out), (gh, gh_buf, gh_out)]
    moves += [tuple(r.at[pl.ds(k * rows, rows)] for r in (gw, gw_buf, gw_out)) for k in range(4)]
    into = [pltpu.make_async_copy(a, b, sems.at[0, k]) for k, (a, b, _) in enumerate(moves)]
    out = [pltpu.make_async_copy(b, d, sems.at[1, k]) for k, (_, b, d) in enumerate(moves)]
    for move in into:
        move.start()
    for first, then in zip(into, out):
        first.wait()
        then.start()
    for move in out:
        move.wait()


def local(states, head_weight, targets, positions, counts, rate_num):
    ndp = lax.axis_size("dp")
    nch = lax.axis_size("vocab")
    ny, nx, nz = ndp // 2, NX, nch // NX
    tokens, d = states.shape
    vw = head_weight.shape[1] // ny
    seq = positions.shape[1]
    rh = LIVE // 4
    first = (rh // 2 + 8) // 16 * 16
    rps = (first, rh - first)
    rgs = [2 * r for r in rps]
    widths = [-(-(r + 1) // 128) * 128 for r in rgs]
    dg = 256 // nch
    cfg = (ny, nx, nz, vw, tokens, seq, ndp * tokens, rps)
    dma = pltpu.SemaphoreType.DMA
    scratch = [
        pltpu.SMEM(counts.shape, jnp.int32),
        pltpu.SMEM(rate_num.shape, jnp.int32),
        pltpu.VMEM(positions.shape, jnp.int32),
        pltpu.VMEM((1, tokens), jnp.int32),
        pltpu.VMEM((2,) + head_weight.shape, BF16),
        pltpu.VMEM((tokens, 128), BF16),
        pltpu.VMEM((tokens, 128), BF16),
        pltpu.VMEM((2, ny, CAP + META, 128), BF16),
        pltpu.VMEM((ndp, 128, vw), BF16),
        *[pltpu.VMEM((nch, r, 128), BF16) for r in rps],
        *[pltpu.VMEM((ny, 2, r, vw), BF16) for r in rps],
        *[pltpu.VMEM((2, ny, r, vw), BF16) for r in rgs],
        *[pltpu.VMEM((2, 2, r, 128), BF16) for r in rps],
        pltpu.VMEM((2, ndp, 128), F32),
        *[pltpu.VMEM((r, META), F32) for r in rgs],
        *[pltpu.VMEM((r, ndp * 128), BF16) for r in rgs],
        *[pltpu.VMEM((ny, 1, w), F32) for w in widths],
        *[pltpu.VMEM((nch, 1, w), F32) for w in widths],
        pltpu.VMEM((2, 1, 128), F32),
        pltpu.VMEM(head_weight.shape, F32),
        *[pltpu.VMEM((256, r), F32) for r in rgs],
        *[pltpu.VMEM((nch, dg, r), F32) for r in rgs],
        pltpu.VMEM((ndp, dg, 128), F32),
        pltpu.VMEM((nch // 2, dg, 128), F32),
        dma((6,)),
        dma((2,)),
        dma,
        dma((ny,)),
        dma((2,)),
        dma((5,)),
        dma((5,)),
        dma((2,)),
        dma,
        dma((2, nz // 2, 2)),
        dma,
        dma((nz,)),
        dma((2,)),
        dma((2,)),
        dma((2, 2, ny // 2, 2)),
        dma((2,)),
        dma((2, ny)),
        dma((2,)),
        dma((2,)),
        dma((2,)),
        dma((2,)),
        dma((2,)),
        dma((2,)),
        dma((2,)),
        dma,
    ]
    vmem = pl.BlockSpec(memory_space=pltpu.VMEM)
    hbm = pl.BlockSpec(memory_space=pltpu.HBM)
    out_shape = (
        jax.ShapeDtypeStruct((1, 1), F32),
        jax.ShapeDtypeStruct((d // nch, tokens), BF16),
        jax.ShapeDtypeStruct(head_weight.shape, F32),
    )
    results = pl.pallas_call(
        functools.partial(kernel, cfg),
        out_shape=out_shape,
        in_specs=[hbm] * 6,
        out_specs=(vmem, vmem, hbm),
        scratch_shapes=scratch,
        compiler_params=pltpu.CompilerParams(
            collective_id=0, has_side_effects=True, vmem_limit_bytes=63 * 1024 * 1024
        ),
    )(counts, rate_num, positions, targets.reshape(1, tokens), states, head_weight)
    loss, grad_hidden, grad_weight = pl.pallas_call(
        copies,
        out_shape=out_shape,
        in_specs=[hbm] * 3,
        out_specs=(hbm,) * 3,
        scratch_shapes=[pltpu.VMEM(o.shape, o.dtype) for o in out_shape] + [dma((2, 6))],
        compiler_params=pltpu.CompilerParams(vmem_limit_bytes=63 * 1024 * 1024),
    )(*results)
    return loss[0, 0], grad_hidden.T, grad_weight


def solution(mesh):
    return jax.shard_map(
        local,
        mesh=mesh,
        in_specs=(P("dp", None), P("dp", "vocab"), P("dp"), P("dp", None), P("dp"), P("dp")),
        out_specs=(P(), P("dp", "vocab"), P("dp", "vocab")),
        check_vma=False,
    )
```
